128 devices in a mesh: ctx: 8 (over x, core), exp: 16 (over z, y).
Axes of the slice: x: 4, y: 4, z: 4, core: 2. Of those that a mesh axis runs over, the one named last changes fastest.
Arguments:
- q_act: bfloat16 [2048, 4096], P('ctx', 'exp'), may hold values from -6 to 6
- k_act: bfloat16 [2048, 4096], P('ctx', 'exp'), may hold values from -6 to 6
- v_act: bfloat16 [2048, 4096], P('ctx', 'exp'), may hold values from -6 to 6
- log_forget: float32 [32, 2048], P('exp', 'ctx'), may hold values from -1 to 0
- attn_gain: float32 [4096], P('exp'), may hold values from 0.1 to 1.9
- w_out: bfloat16 [4096, 6144], P('exp'), may hold values from -0.09375 to 0.09375
- resid: bfloat16 [2048, 6144], P(('ctx', 'exp')), may hold values from -6 to 6
- mlp_gain: float32 [6144], replicated, may hold values from 0.1 to 1.9
- gate_w: bfloat16 [16, 4608, 6144], P('exp', 'ctx'), may hold values from -0.078125 to 0.078125
- up_w: bfloat16 [16, 4608, 6144], P('exp', 'ctx'), may hold values from -0.078125 to 0.078125
- down_w: bfloat16 [16, 4608, 6144], P('exp', 'ctx'), may hold values from -0.0625 to 0.0625
- expert_ids: int32 [2048, 2], P(('ctx', 'exp')), may hold values from 0 to 7, all different within a row; in each aligned block of 16 rows (0 to 15, 16 to 31, ...) at most 6 rows name the same one
- gate_codes: int32 [2048, 2], P(('ctx', 'exp')), may hold values from 1 to 1023
Outputs:
- layer_out: bfloat16 [2048, 6144], P(('ctx', 'exp'))
The draws below stay inside these ranges and needn't reach their ends.
Inputs may be any that keep to these rules, and one draw needn't show every extreme that they name: `expert_ids`: each row names two different experts. In the rows of one device (aligned blocks of 16 rows) no expert is named more than 6 times.
All inputs are finite; a program needn't handle non-finite values.
Results may differ from the reference program's by a relative error of at most 0.02.
Values may be sent and summed in bfloat16 or wider, within the bound.
No kernel may reach another device: no remote copies, remote signals or barrier semaphores. Data moves between devices by JAX's collectives and lax.ppermute only.
A program may use at most 128 MiB of HBM per device.

```python
import math
import jax
import jax.numpy as jnp
import numpy as np
from jax import lax

D = 6144
HEADS = 32
HEAD_DIM = 128
FF = 9216
EXPERTS = 8
TOP = 2
BLOCK = 256
STREAM_LENGTH = 2048
TOK_DEV = 16
SPLIT = 2
CAP = 6
FF_DEV = 576
N_EXP = 16


def draw_log_forget(key, part):
    key = jax.random.fold_in(key, 7)
    key_kind, key_base, key_rough, random_seed_handle, key_loss = jax.random.split(key, 5)
    fast_share = 0.5
    chooser = jax.random.uniform(key_kind, (HEADS, 1), jnp.float32)
    fast_rate = -1.0 / jax.random.uniform(key_base, (HEADS, 1), jnp.float32, 30.0, 50.0)
    slow_rate = jnp.full((HEADS, 1), -0.5 / STREAM_LENGTH, jnp.float32)
    default_forget_speed = jnp.where(chooser < fast_share, fast_rate, slow_rate)
    jagged_perturbation = jnp.exp(jax.random.uniform(key_rough, (HEADS, STREAM_LENGTH), jnp.float32, -0.7, 0.7))
    spike_index_entry = jax.random.randint(random_seed_handle, (2,), 0, STREAM_LENGTH)
    objective_figures = jnp.log(1.0 - jax.random.uniform(key_loss, (HEADS, 2), jnp.float32, 0.2, 0.5))
    element_indices = jnp.arange(STREAM_LENGTH)
    spike_occurrences = jnp.where(element_indices[None, :] == spike_index_entry[0], objective_figures[:, 0:1], 0.0)
    spike_occurrences = spike_occurrences + jnp.where(element_indices[None, :] == spike_index_entry[1], objective_figures[:, 1:2], 0.0)
    return (default_forget_speed * jagged_perturbation + spike_occurrences).astype(jnp.float32)


def with_ends(array, stream_key, low, largest):
    dims = array.shape
    place = [jax.random.randint(jax.random.fold_in(stream_key, axis), (), 0, dims[axis]) for axis in range(len(dims))]
    array = array.at[tuple(place)].set(low)
    longest = dims.index(max(dims))
    place[longest] = (place[longest] + 1) % dims[longest]
    return array.at[tuple(place)].set(largest)


def steps_of(rng, dims, cuts, smallest, largest):
    def one(axis_at, blocks):
        heights = jax.random.uniform(jax.random.fold_in(jax.random.fold_in(rng, 6), axis_at), (blocks,), jnp.float32, smallest / len(cuts), largest / len(cuts))
        return jnp.repeat(jnp.exp(heights), dims[axis_at] // blocks).reshape((-1,) + (1,) * (len(dims) - axis_at - 1))

    loudness = one(*cuts[0])
    for cut in cuts[1:]:
        loudness = loudness * one(*cut)
    return loudness


def deal_out(own_key, own, number, rows, number_of, top, reach, slope):
    order = jax.random.permutation(own_key, number_of)
    packed, usual = portions_of(number_of, rows * top, reach, slope, True), portions_of(number_of, rows * top, reach, slope, False)
    places = jnp.arange(number_of)

    def named(lengths, turn):
        used = int((lengths > 0).sum())
        fixed = max(1, used // 4)
        shifted = fixed + (places - fixed + turn * (used - fixed)) % max(1, number_of - fixed)
        return jnp.zeros((number_of,), jnp.int32).at[order[jnp.where(places < fixed, places, shifted)]].set(jnp.asarray(lengths, jnp.int32))

    lengths = jnp.where(number % 4 == 0, named(packed, number // 4), named(usual, number - number // 4 - 1))
    mixed = jax.random.permutation(jax.random.fold_in(own, 3), number_of)
    source_of, taker = mixed[0:number_of // 2 * 2:2], mixed[1:number_of // 2 * 2:2]
    margin = jnp.minimum(lengths[source_of] - 1, reach - lengths[taker]) // 2
    margin = jnp.where((source_of == order[0]) | (taker == order[0]) | (lengths[taker] == 0), 0, jnp.maximum(margin, 0))
    shifted = jax.random.randint(jax.random.fold_in(own, 4), (number_of // 2,), 0, 1 << 20) % (margin + 1)
    lengths = lengths.at[source_of].add(-shifted).at[taker].add(shifted)
    items = jnp.searchsorted(jnp.cumsum(lengths), jnp.arange(rows * top), side="right").astype(jnp.int32)
    grid = items.reshape(top, rows).T
    grid = grid[jax.random.permutation(jax.random.fold_in(own, 1), rows)]
    turn = jax.random.randint(jax.random.fold_in(own, 2), (rows, 1), 0, top)
    return jnp.take_along_axis(grid, (jnp.arange(top)[None, :] + turn) % top, axis=1)


def portions_of(amount, total, bound, lean, full):
    portions = [(1 << 20) // math.isqrt(grade ** lean) + 1 for grade in range(1, amount + 1)]
    largest = bound if full else min(bound, max(-(-total // amount), total * portions[0] // sum(portions)))
    least = 1 if total - largest >= amount - 1 else 0
    counts, surplus = [largest] + [least] * (amount - 1), total - largest - least * (amount - 1)
    while surplus > 0:
        movable = [i for i in range(1, amount) if counts[i] < largest] or [i for i in range(1, amount) if counts[i] < bound]
        pool, left = sum([portions[i] for i in movable]), surplus
        for i in movable:
            extra = min(bound - counts[i], max(1, left * portions[i] // pool), surplus)
            counts[i] = counts[i] + extra
            surplus = surplus - extra
    return np.array(counts)


def noise(key, extent, scale, limit, cuts=(), kind=jnp.bfloat16):
    factor_of = steps_of(key, extent, cuts, -0.22, 0.18) if cuts else 1.0
    values = jax.random.normal(key, extent, jnp.float32) * scale * factor_of
    return jnp.minimum(jnp.maximum(values, -limit), limit).astype(kind)


def setup_inputs(seed: int = 0) -> dict:
    key_list = jax.random.split(jax.random.key(seed), 14)
    q_act = noise(key_list[0], (STREAM_LENGTH, HEADS * HEAD_DIM), 1.0, 6.0, ((0, 8), (1, 16)))
    k_act = noise(key_list[1], (STREAM_LENGTH, HEADS * HEAD_DIM), 1.0, 6.0, ((0, 8), (1, 16)))
    v_act = noise(key_list[2], (STREAM_LENGTH, HEADS * HEAD_DIM), 1.0, 6.0, ((0, 8), (1, 16)))
    log_forget = draw_log_forget(jax.random.fold_in(key_list[13], 71), 0)
    attn_gain = jnp.clip(1.0 + 0.18 * jax.random.normal(key_list[4], (HEADS * HEAD_DIM,), jnp.float32), 0.1, 1.9)
    w_out = noise(key_list[5], (HEADS * HEAD_DIM, D), (HEADS * HEAD_DIM) ** -0.5, 0.09375, ((0, 16),))
    resid = noise(key_list[6], (STREAM_LENGTH, D), 1.0, 6.0, ((0, 128),))
    mlp_gain = jnp.clip(1.0 + 0.18 * jax.random.normal(key_list[7], (D,), jnp.float32), 0.1, 1.9)
    gate_w = noise(key_list[8], (N_EXP, FF // SPLIT, D), D ** -0.5, 0.078125, ((0, 16), (1, 8)))
    up_w = noise(key_list[9], (N_EXP, FF // SPLIT, D), D ** -0.5, 0.078125, ((0, 16), (1, 8)))
    down_w = noise(key_list[10], (N_EXP, FF // SPLIT, D), FF ** -0.5, 0.0625, ((0, 16), (1, 8)))
    expert_ids_keys = jax.random.split(jax.random.fold_in(key_list[11], 1), STREAM_LENGTH // TOK_DEV)
    expert_ids_turns = jax.random.permutation(jax.random.fold_in(key_list[11], 3), STREAM_LENGTH // TOK_DEV)
    expert_ids = jax.vmap(lambda own, number: deal_out(jax.random.fold_in(key_list[11], 2), own, number, TOK_DEV, EXPERTS, TOP, CAP, 2))(expert_ids_keys, expert_ids_turns).reshape((STREAM_LENGTH, TOP))
    gate_codes = with_ends(jax.random.randint(key_list[12], (STREAM_LENGTH, TOP), 1, 1024), jax.random.fold_in(key_list[12], 1), 1, 1023).astype(jnp.int32)
    return {"q_act": q_act, "k_act": k_act, "v_act": v_act, "log_forget": log_forget, "attn_gain": attn_gain, "w_out": w_out, "resid": resid, "mlp_gain": mlp_gain, "gate_w": gate_w, "up_w": up_w, "down_w": down_w, "expert_ids": expert_ids, "gate_codes": gate_codes}


EPS = 1e-06

def slot_tables(ids, codes, experts, capacity):
    rows = ids.shape[0]
    width = ids.shape[1]
    flat = ids.reshape(-1)
    onehot = (flat[:, None] == jnp.arange(experts, dtype=jnp.int32)[None, :]).astype(jnp.int32)
    before = jnp.cumsum(onehot, axis=0) - onehot
    slot = lax.optimization_barrier(jnp.sum(before * onehot, axis=1))
    target = (flat * capacity + slot).astype(jnp.int32)
    assign = (target[None, :] == jnp.arange(experts * capacity, dtype=jnp.int32)[:, None]).astype(jnp.float32)
    assign = assign.reshape(experts * capacity, rows, width)
    dispatch = lax.optimization_barrier(jnp.sum(assign, axis=2))
    route = codes.astype(jnp.float32)
    route = route / lax.optimization_barrier(jnp.sum(route, axis=1, keepdims=True))
    combine = jnp.einsum('srk,rk->rs', assign, route, precision=lax.Precision.HIGHEST)
    return (dispatch, combine)

def head_attention(query_rows, key_rows, value_rows, rates):
    scale = HEAD_DIM ** (-0.5)
    nblocks = STREAM_LENGTH // BLOCK
    positions = jnp.arange(BLOCK)
    causal = positions[:, None] >= positions[None, :]

    def advance(state, pieces):
        qh, kh, vh, rate_blk = pieces
        cumul = jnp.cumsum(rate_blk)
        differ = jnp.where(causal, cumul[:, None] - cumul[None, :], 0.0)
        decay = jnp.where(causal, jnp.exp(differ), 0.0)
        scores = jnp.dot(qh, kh.T, preferred_element_type=jnp.float32) * scale * decay
        intra = jnp.dot(scores.astype(jnp.bfloat16), vh, preferred_element_type=jnp.float32)
        inter = scale * jnp.exp(cumul)[:, None] * jnp.dot(qh.astype(jnp.float32), state, precision=lax.Precision.HIGHEST)
        fading = jnp.exp(cumul[-1] - cumul)
        update = jnp.dot((kh.astype(jnp.float32) * fading[:, None]).T, vh.astype(jnp.float32), precision=lax.Precision.HIGHEST)
        state = jnp.exp(cumul[-1]) * state + update
        return (state, intra + inter)
    start_state = jnp.zeros((HEAD_DIM, HEAD_DIM), jnp.float32)
    pieces = (query_rows.reshape(nblocks, BLOCK, HEAD_DIM), key_rows.reshape(nblocks, BLOCK, HEAD_DIM), value_rows.reshape(nblocks, BLOCK, HEAD_DIM), rates.reshape(nblocks, BLOCK))
    final_state, outputs = lax.scan(advance, start_state, pieces)
    return outputs.reshape(STREAM_LENGTH, HEAD_DIM)

def reference(q_act, k_act, v_act, log_forget, attn_gain, w_out, resid, mlp_gain, gate_w, up_w, down_w, expert_ids, gate_codes):
    queries = q_act.reshape(STREAM_LENGTH, HEADS, HEAD_DIM).transpose(1, 0, 2)
    keys_all = k_act.reshape(STREAM_LENGTH, HEADS, HEAD_DIM).transpose(1, 0, 2)
    values_all = v_act.reshape(STREAM_LENGTH, HEADS, HEAD_DIM).transpose(1, 0, 2)
    heads_out = lax.map(lambda t: head_attention(t[0], t[1], t[2], t[3]), (queries, keys_all, values_all, log_forget))
    meansq = lax.optimization_barrier(jnp.mean(heads_out * heads_out, axis=2, keepdims=True))
    normed = heads_out * lax.rsqrt(meansq + EPS)
    attn_out = (normed.transpose(1, 0, 2).reshape(STREAM_LENGTH, HEADS * HEAD_DIM) * attn_gain).astype(jnp.bfloat16)
    proj = jnp.dot(attn_out, w_out, preferred_element_type=jnp.float32)
    mid = (resid.astype(jnp.float32) + proj).astype(jnp.bfloat16)
    mid_f = mid.astype(jnp.float32)
    mixed_in = (mid_f * lax.rsqrt(lax.optimization_barrier(jnp.mean(mid_f * mid_f, axis=1, keepdims=True)) + EPS) * mlp_gain).astype(jnp.bfloat16)
    ndev = STREAM_LENGTH // TOK_DEV
    ids = expert_ids.reshape(ndev, TOK_DEV, TOP)
    codes = gate_codes.reshape(ndev, TOK_DEV, TOP)
    dispatch, combine = jax.vmap(lambda a, b: slot_tables(a, b, EXPERTS, CAP))(ids, codes)
    tokens_dev = mixed_in.astype(jnp.float32).reshape(ndev, TOK_DEV, D)
    slots = jnp.einsum('dst,dtc->dsc', dispatch, tokens_dev, precision=lax.Precision.HIGHEST).astype(jnp.bfloat16)
    slots = slots.reshape(ndev, EXPERTS, CAP, D).transpose(1, 0, 2, 3).reshape(EXPERTS, ndev * CAP, D)
    pieces = FF // FF_DEV

    def expert_fn(index):
        rows_in = slots[index]
        gate_m = lax.dynamic_slice_in_dim(gate_w, index * SPLIT, SPLIT, 0).reshape(FF, D)
        up_m = lax.dynamic_slice_in_dim(up_w, index * SPLIT, SPLIT, 0).reshape(FF, D)
        down_m = lax.dynamic_slice_in_dim(down_w, index * SPLIT, SPLIT, 0).reshape(FF, D)
        gate = jnp.dot(rows_in, gate_m.T, preferred_element_type=jnp.float32)
        upper = jnp.dot(rows_in, up_m.T, preferred_element_type=jnp.float32)
        hidden = (jax.nn.silu(gate) * upper).astype(jnp.bfloat16)

        def add_piece(total, number):
            part_h = lax.dynamic_slice_in_dim(hidden, number * FF_DEV, FF_DEV, 1)
            part_w = lax.dynamic_slice_in_dim(down_m, number * FF_DEV, FF_DEV, 0)
            term = lax.optimization_barrier(jnp.dot(part_h, part_w, preferred_element_type=jnp.float32).astype(jnp.bfloat16))
            return (total + term.astype(jnp.float32), None)
        total, unused = lax.scan(add_piece, jnp.zeros((ndev * CAP, D), jnp.float32), jnp.arange(pieces, dtype=jnp.int32))
        return total
    outputs = lax.map(expert_fn, jnp.arange(EXPERTS, dtype=jnp.int32))
    outputs = outputs.reshape(EXPERTS, ndev, CAP, D).transpose(1, 0, 2, 3).reshape(ndev, EXPERTS * CAP, D)
    moe = jnp.einsum('dts,dsc->dtc', combine, outputs, precision=lax.Precision.HIGHEST).reshape(STREAM_LENGTH, D)
    return (mid_f + moe).astype(jnp.bfloat16)
```

```python
import jax
import jax.numpy as jnp
from jax import lax
from jax.experimental import pallas as pl
from jax.experimental.pallas import tpu as pltpu
from jax.sharding import PartitionSpec as P

D = 6144
HEAD_DIM = 128
EXPERTS = 8
BLOCK = 256
N_CTX = 8
N_EXP = 16
RING = 4
CAP = 6
ROWS = N_EXP * CAP
HALF = ROWS // 2
COLS = D // N_EXP
EPS = 1e-06
F32 = jnp.float32
BF16 = jnp.bfloat16
VMEM_BYTES = 56 * 1024 * 1024


def along_x(value, steps):
    pairs = [(c, ((c // 2 + steps) % RING) * 2 + c % 2) for c in range(N_CTX)]
    return lax.ppermute(value, "ctx", pairs)


def other_core(value):
    return lax.ppermute(value, "ctx", [(c, c ^ 1) for c in range(N_CTX)])


def forward(value, steps):
    return lax.ppermute(value, "ctx", [(c, c + steps) for c in range(N_CTX - steps)])


def all_to_all_exp(value):
    return lax.all_to_all(value, "exp", split_axis=0, concat_axis=0, tiled=True)


def three_parts(x):
    a = lax.reduce_precision(x, 8, 7)
    b = lax.reduce_precision(x - a, 8, 7)
    c = lax.reduce_precision(x - a - b, 8, 7)
    return a, b, c


def attention(q_act, k_act, v_act, log_forget, attn_gain):
    heads = log_forget.shape[0]
    rows = q_act.shape[0]
    scale = HEAD_DIM ** (-0.5)
    query = q_act.reshape(rows, heads, HEAD_DIM)
    key = k_act.reshape(rows, heads, HEAD_DIM)
    value = v_act.reshape(rows, heads, HEAD_DIM)
    cumul = jnp.cumsum(log_forget, axis=1)
    ends = cumul[:, -1]
    fading = jnp.exp(ends[:, None] - cumul).T
    key_faded = key.astype(F32) * fading[..., None]
    update = jnp.einsum(
        "jhd,jhe->hde", key_faded, value.astype(F32), precision=lax.Precision.HIGHEST
    )
    parts = jnp.stack(three_parts(ends), axis=0).reshape(-1)
    parts = jnp.broadcast_to(
        jnp.pad(parts, (0, 16 - parts.shape[0]))[:, None], (16, HEAD_DIM)
    )
    packed = jnp.concatenate(
        [update.reshape(heads * HEAD_DIM, HEAD_DIM), parts], axis=0
    ).astype(BF16)
    incoming = jnp.zeros((heads, HEAD_DIM, HEAD_DIM), F32)
    passed = jnp.zeros((heads,), F32)
    for steps in range(1, N_CTX):
        got = forward(packed, steps).astype(F32)
        state = got[: heads * HEAD_DIM].reshape(heads, HEAD_DIM, HEAD_DIM)
        incoming = incoming + jnp.exp(passed)[:, None, None] * state
        logs = got[heads * HEAD_DIM : heads * HEAD_DIM + 3 * heads, 0].reshape(3, heads)
        passed = passed + (logs[0] + logs[1] + logs[2])
    positions = jnp.arange(rows)
    causal = positions[:, None] >= positions[None, :]
    differ = jnp.where(causal, cumul[:, :, None] - cumul[:, None, :], 0.0)
    decay = jnp.where(causal, jnp.exp(differ), 0.0)
    scores = (
        jnp.einsum("ihd,jhd->hij", query, key, preferred_element_type=F32) * scale * decay
    )
    intra = jnp.einsum("hij,jhd->hid", scores.astype(BF16), value, preferred_element_type=F32)
    inter = jnp.einsum(
        "ihd,hde->hie", query.astype(F32), incoming, precision=lax.Precision.HIGHEST
    )
    heads_out = intra + scale * jnp.exp(cumul)[..., None] * inter
    meansq = jnp.mean(heads_out * heads_out, axis=2, keepdims=True)
    normed = heads_out * lax.rsqrt(meansq + EPS)
    normed = normed.transpose(1, 0, 2).reshape(rows, heads * HEAD_DIM)
    return (normed * attn_gain).astype(BF16)


def slot_targets(ids):
    flat = ids.reshape(-1)
    onehot = (flat[:, None] == jnp.arange(EXPERTS, dtype=jnp.int32)[None, :]).astype(jnp.int32)
    before = jnp.cumsum(onehot, axis=0) - onehot
    slot = jnp.sum(before * onehot, axis=1)
    return slot.reshape(ids.shape)


def proj_body(a_ref, w_ref, resid_ref, hot_ref, mid_ref, send_ref, acc):
    step = pl.program_id(0)
    part = jnp.dot(
        a_ref[0], w_ref[...].reshape(BLOCK, COLS), preferred_element_type=F32
    )

    @pl.when(step == 0)
    def _():
        acc[...] = part

    @pl.when(step > 0)
    def _():
        acc[...] += part

    @pl.when(step == N_EXP - 1)
    def _():
        mid = (resid_ref[...].astype(F32) + acc[...]).astype(BF16)
        mid_ref[...] = mid
        send_ref[...] = jnp.dot(hot_ref[...], mid, preferred_element_type=F32).astype(BF16)


def project(gathered, w_cols, resid_cols, hot):
    return pl.pallas_call(
        proj_body,
        grid=(N_EXP,),
        in_specs=[
            pl.BlockSpec((1, BLOCK, 256), lambda j: (j, 0, 0)),
            pl.BlockSpec((N_CTX, 1, 32, COLS), lambda j: (0, j, 0, 0)),
            pl.BlockSpec((BLOCK, COLS), lambda j: (0, 0)),
            pl.BlockSpec((N_EXP * ROWS, BLOCK), lambda j: (0, 0)),
        ],
        out_specs=[
            pl.BlockSpec((BLOCK, COLS), lambda j: (0, 0)),
            pl.BlockSpec((N_EXP * ROWS, COLS), lambda j: (0, 0)),
        ],
        out_shape=[
            jax.ShapeDtypeStruct((BLOCK, COLS), BF16),
            jax.ShapeDtypeStruct((N_EXP * ROWS, COLS), BF16),
        ],
        scratch_shapes=[pltpu.VMEM((BLOCK, COLS), F32)],
        compiler_params=pltpu.CompilerParams(vmem_limit_bytes=VMEM_BYTES),
        cost_estimate=pl.CostEstimate(
            flops=2 * BLOCK * 4096 * COLS, bytes_accessed=10_000_000, transcendentals=0
        ),
        name="project",
    )(gathered, w_cols, resid_cols, hot)


def norm_body(got_ref, gain_ref, *out_refs):
    for half, out_ref in enumerate(out_refs):
        rows = pl.ds(half * HALF, HALF)
        total = jnp.zeros((HALF, 1), F32)
        for j in range(N_EXP):
            piece = got_ref[j, rows, :].astype(F32)
            total += jnp.sum(piece * piece, axis=1, keepdims=True)
        factor = lax.rsqrt(total * (1.0 / D) + EPS)
        for j in range(N_EXP):
            cols = pl.ds(j * COLS, COLS)
            piece = got_ref[j, rows, :].astype(F32)
            out_ref[:, cols] = (piece * factor * gain_ref[:, cols]).astype(BF16)


def norm_rows(got, mlp_gain):
    return pl.pallas_call(
        norm_body,
        in_specs=[pl.BlockSpec(memory_space=pltpu.VMEM)] * 2,
        out_specs=[pl.BlockSpec(memory_space=pltpu.VMEM)] * 2,
        out_shape=[jax.ShapeDtypeStruct((HALF, D), BF16)] * 2,
        compiler_params=pltpu.CompilerParams(vmem_limit_bytes=VMEM_BYTES),
        cost_estimate=pl.CostEstimate(
            flops=4 * ROWS * D, bytes_accessed=4 * ROWS * D, transcendentals=0
        ),
        name="norm_rows",
    )(got, mlp_gain.reshape(1, D))


STEPS = 6
WIDE = D // STEPS


def ffn_body(*refs):
    n = 2 * RING
    x_refs = refs[:n]
    gate_ref, up_ref, down_ref = refs[n : n + 3]
    out_refs = refs[n + 3 : 2 * n + 3]
    gate_acc, up_acc, hidden = refs[2 * n + 3 :]
    step = pl.program_id(0)
    dims = (((1,), (1,)), ((), ()))

    @pl.when(step < STEPS)
    def _():
        rows = jnp.concatenate([r[...] for r in x_refs], axis=0)
        gate = lax.dot_general(rows, gate_ref[0], dims, preferred_element_type=F32)
        up = lax.dot_general(rows, up_ref[0], dims, preferred_element_type=F32)

        @pl.when(step == 0)
        def _():
            gate_acc[...] = gate
            up_acc[...] = up

        @pl.when(step > 0)
        def _():
            gate_acc[...] += gate
            up_acc[...] += up

    @pl.when(step == STEPS - 1)
    def _():
        hidden[...] = (jax.nn.silu(gate_acc[...]) * up_acc[...]).astype(BF16)

    @pl.when(step >= STEPS)
    def _():
        out = jnp.dot(hidden[...], down_ref[0], preferred_element_type=F32).astype(BF16)
        for i, out_ref in enumerate(out_refs):
            out_ref[...] = out[i * HALF : (i + 1) * HALF]


def expert_ffn(pieces, gate_w, up_w, down_w):
    n = 2 * RING
    total = n * HALF
    ff = gate_w.shape[1]
    first = lambda i: jnp.minimum(i, STEPS - 1)
    second = lambda i: jnp.maximum(i - STEPS, 0)
    return pl.pallas_call(
        ffn_body,
        grid=(2 * STEPS,),
        in_specs=[pl.BlockSpec((HALF, WIDE), lambda i: (0, first(i)))] * n
        + [pl.BlockSpec((1, ff, WIDE), lambda i: (0, 0, first(i)))] * 2
        + [pl.BlockSpec((1, ff, WIDE), lambda i: (0, 0, second(i)))],
        out_specs=[pl.BlockSpec((HALF, WIDE), lambda i: (0, second(i)))] * n,
        out_shape=[jax.ShapeDtypeStruct((HALF, D), BF16)] * n,
        scratch_shapes=[
            pltpu.VMEM((total, ff), F32),
            pltpu.VMEM((total, ff), F32),
            pltpu.VMEM((total, ff), BF16),
        ],
        compiler_params=pltpu.CompilerParams(vmem_limit_bytes=VMEM_BYTES),
        cost_estimate=pl.CostEstimate(
            flops=6 * total * ff * D,
            bytes_accessed=6 * ff * D + 4 * total * D,
            transcendentals=total * ff,
        ),
        name="expert_ffn",
    )(*pieces, gate_w, up_w, down_w)


def gather_rows(own, way):
    left = along_x(own, 1)
    right = along_x(own, -1)
    far = along_x(left, 1) if way > 0 else along_x(right, -1)
    mine = [own, left, right, far]
    return mine + [other_core(piece) for piece in mine]


def added(*terms):
    total = terms[0].astype(F32)
    for term in terms[1:]:
        total = total + term.astype(F32)
    return total


def scatter_rows(outs, way):
    theirs = [other_core(piece) for piece in outs[RING:]]
    own, left, right, far = [added(a, b) for a, b in zip(outs[:RING], theirs)]
    far = far.astype(BF16)
    if way > 0:
        right = right + along_x(far, 1).astype(F32)
    else:
        left = left + along_x(far, -1).astype(F32)
    from_left = along_x(right.astype(BF16), 1)
    from_right = along_x(left.astype(BF16), -1)
    return added(own, from_left, from_right).astype(BF16)


def shards(
    q_act,
    k_act,
    v_act,
    log_forget,
    attn_gain,
    w_out,
    resid,
    mlp_gain,
    gate_w,
    up_w,
    down_w,
    expert_ids,
    gate_codes,
):
    tok_dev = resid.shape[0]
    slot = slot_targets(expert_ids)
    place = expert_ids * ROWS + lax.axis_index("exp") * CAP + slot
    places = lax.all_gather(place, "exp", axis=0, tiled=True)
    targets = jnp.arange(N_EXP * ROWS, dtype=jnp.int32)
    targets = (targets // (2 * ROWS)) * ROWS + targets % ROWS
    hot = (
        (targets[:, None] == places[None, :, 0]) | (targets[:, None] == places[None, :, 1])
    ).astype(BF16)

    eighth = w_out.shape[0] // N_CTX
    w_part = lax.dynamic_slice_in_dim(w_out, lax.axis_index("ctx") * eighth, eighth, 0)
    early = jnp.concatenate([w_part, resid], axis=0)
    early = early.reshape(eighth + tok_dev, N_EXP, COLS).transpose(1, 0, 2)
    early = all_to_all_exp(early)
    resid_cols = early[:, eighth:].reshape(N_EXP * tok_dev, COLS)
    w_cols = lax.all_gather(early[:, :eighth], "ctx", axis=0)

    attn_out = attention(q_act, k_act, v_act, log_forget, attn_gain)
    gathered = all_to_all_exp(jnp.broadcast_to(attn_out[None], (N_EXP,) + attn_out.shape))
    mid_cols, send = project(gathered, w_cols, resid_cols, hot)
    got = all_to_all_exp(send.reshape(N_EXP, ROWS, COLS))
    halves = norm_rows(got, mlp_gain)
    mid_own = all_to_all_exp(mid_cols.reshape(N_EXP, tok_dev, COLS))

    sums = []
    for way, half in zip((1, -1), halves):
        outs = expert_ffn(gather_rows(half, way), gate_w, up_w, down_w)
        sums.append(scatter_rows(outs, way))
    back = jnp.concatenate(sums, axis=0).reshape(N_EXP, CAP, D)
    returned = all_to_all_exp(back).astype(F32)
    outputs = jnp.sum(returned.reshape(EXPERTS, 2, CAP, D), axis=1).reshape(EXPERTS * CAP, D)

    own_place = (expert_ids * CAP + slot)[:, :, None]
    route = gate_codes.astype(F32)
    route = route / jnp.sum(route, axis=1, keepdims=True)
    slots = jnp.arange(EXPERTS * CAP, dtype=jnp.int32)[None, None, :]
    combine = jnp.sum(jnp.where(own_place == slots, route[:, :, None], 0.0), axis=1)
    moe = jnp.dot(combine, outputs, precision=lax.Precision.HIGHEST, preferred_element_type=F32)
    mid_f = mid_own.transpose(1, 0, 2).reshape(tok_dev, D).astype(F32)
    return (mid_f + moe).astype(BF16)


def solution(mesh):
    placed = (
        P("ctx", "exp"),
        P("ctx", "exp"),
        P("ctx", "exp"),
        P("exp", "ctx"),
        P("exp"),
        P("exp", None),
        P(("ctx", "exp"), None),
        P(),
        P("exp", "ctx", None),
        P("exp", "ctx", None),
        P("exp", "ctx", None),
        P(("ctx", "exp"), None),
        P(("ctx", "exp"), None),
    )
    return jax.shard_map(
        shards, mesh=mesh, in_specs=placed, out_specs=P(("ctx", "exp"), None), check_vma=False
    )
```

```python
import jax
import jax.numpy as jnp
from jax import lax
from jax.experimental import pallas as pl
from jax.experimental.pallas import tpu as pltpu
from jax.sharding import PartitionSpec as P

D = 6144
HEAD_DIM = 128
EXPERTS = 8
BLOCK = 256
N_CTX = 8
N_EXP = 16
RING = 4
CAP = 6
ROWS = N_EXP * CAP
HALF = ROWS // 2
COLS = D // N_EXP
EIGHTH = 256 // N_CTX
EPS = 1e-06
F32 = jnp.float32
BF16 = jnp.bfloat16
VMEM_BYTES = 24 * 1024 * 1024
LIGHT = dict(flops=1000, bytes_accessed=1000, transcendentals=0)


def along_x(value, steps):
    pairs = [(c, ((c // 2 + steps) % RING) * 2 + c % 2) for c in range(N_CTX)]
    return lax.ppermute(value, "ctx", pairs)


def other_core(value):
    return lax.ppermute(value, "ctx", [(c, c ^ 1) for c in range(N_CTX)])


def along_y(value, steps):
    pairs = [(j, j // RING * RING + (j % RING + steps) % RING) for j in range(N_EXP)]
    return lax.ppermute(value, "exp", pairs)


def along_z(value, steps):
    pairs = [(j, (j + RING * steps) % N_EXP) for j in range(N_EXP)]
    return lax.ppermute(value, "exp", pairs)


def next_chips(value, steps):
    pairs = [(c, c + 2 * steps) for c in range(N_CTX - 2 * steps)]
    return lax.ppermute(value, "ctx", pairs)


def all_to_all_exp(value):
    return lax.all_to_all(value, "exp", split_axis=0, concat_axis=0, tiled=True)


def three_parts(x):
    a = lax.reduce_precision(x, 8, 7)
    b = lax.reduce_precision(x - a, 8, 7)
    c = lax.reduce_precision(x - a - b, 8, 7)
    return a, b, c


def attention(q_act, k_act, v_act, log_forget, attn_gain):
    heads = log_forget.shape[0]
    rows = q_act.shape[0]
    scale = HEAD_DIM ** (-0.5)
    query = q_act.reshape(rows, heads, HEAD_DIM)
    key = k_act.reshape(rows, heads, HEAD_DIM)
    value = v_act.reshape(rows, heads, HEAD_DIM)
    cumul = jnp.cumsum(log_forget, axis=1)
    ends = cumul[:, -1]
    fading = jnp.exp(ends[:, None] - cumul).T
    key_faded = key.astype(F32) * fading[..., None]
    update = jnp.einsum(
        "jhd,jhe->hde", key_faded, value.astype(F32), precision=lax.Precision.HIGHEST
    )
    def packed(state, log):
        parts = jnp.stack(three_parts(log), axis=0).reshape(-1)
        parts = jnp.pad(parts, (0, 16 - parts.shape[0]))
        parts = jnp.broadcast_to(parts[:, None], (16, HEAD_DIM))
        return jnp.concatenate([state.reshape(heads * HEAD_DIM, HEAD_DIM), parts]).astype(BF16)

    def unpacked(got):
        got = got.astype(F32)
        state = got[: heads * HEAD_DIM].reshape(heads, HEAD_DIM, HEAD_DIM)
        logs = got[heads * HEAD_DIM : heads * HEAD_DIM + 3 * heads, 0].reshape(3, heads)
        return state, logs[0] + logs[1] + logs[2]

    grown = lambda log: jnp.exp(log)[:, None, None]
    second = lax.axis_index("ctx") % 2 == 1
    mate, mate_log = unpacked(other_core(packed(update, ends)))
    chip = jnp.where(second, grown(ends) * mate + update, grown(mate_log) * update + mate)
    chip = packed(chip, ends + mate_log)
    incoming = jnp.zeros((heads, HEAD_DIM, HEAD_DIM), F32)
    before = jnp.zeros((heads,), F32)
    arrived = [next_chips(chip, steps) for steps in range(1, RING)]
    for got in arrived:
        state, log = unpacked(got)
        incoming = incoming + grown(before) * state
        before = before + log
    incoming = jnp.where(second, grown(mate_log) * incoming + mate, incoming)
    positions = jnp.arange(rows)
    causal = positions[:, None] >= positions[None, :]
    differ = jnp.where(causal, cumul[:, :, None] - cumul[:, None, :], 0.0)
    decay = jnp.where(causal, jnp.exp(differ), 0.0)
    scores = (
        jnp.einsum("ihd,jhd->hij", query, key, preferred_element_type=F32) * scale * decay
    )
    intra = jnp.einsum("hij,jhd->hid", scores.astype(BF16), value, preferred_element_type=F32)
    inter = jnp.einsum(
        "ihd,hde->hie", query.astype(F32), incoming, precision=lax.Precision.HIGHEST
    )
    heads_out = intra + scale * jnp.exp(cumul)[..., None] * inter
    meansq = jnp.mean(heads_out * heads_out, axis=2, keepdims=True)
    normed = heads_out * lax.rsqrt(meansq + EPS)
    normed = normed.transpose(1, 0, 2).reshape(rows, heads * HEAD_DIM)
    return (normed * attn_gain).astype(BF16), chip, arrived


def slot_targets(ids):
    flat = ids.reshape(-1)
    onehot = (flat[:, None] == jnp.arange(EXPERTS, dtype=jnp.int32)[None, :]).astype(jnp.int32)
    before = jnp.cumsum(onehot, axis=0) - onehot
    slot = jnp.sum(before * onehot, axis=1)
    return slot.reshape(ids.shape)


def partial_body(*refs):
    a_refs, w_refs = refs[:RING], refs[RING : RING + N_CTX]
    out_refs = refs[RING + N_CTX :]
    for out_ref, k in zip(out_refs, (2, 1, 3, 0)):
        cols = pl.ds(k * COLS, COLS)
        total = None
        for d, a_ref in enumerate(a_refs):
            rows = pl.ds(d * EIGHTH, EIGHTH)
            weight = jnp.concatenate([w_ref[rows, cols] for w_ref in w_refs], axis=0)
            part = jnp.dot(a_ref[...], weight, preferred_element_type=F32)
            total = part if total is None else total + part
        out_ref[...] = total.astype(BF16)


def partial_sums(a_pieces, w_pieces):
    return pl.pallas_call(
        partial_body,
        in_specs=[pl.BlockSpec(memory_space=pltpu.VMEM)] * (RING + N_CTX),
        out_specs=[pl.BlockSpec(memory_space=pltpu.VMEM)] * RING,
        out_shape=[jax.ShapeDtypeStruct((BLOCK, COLS), BF16)] * RING,
        compiler_params=pltpu.CompilerParams(vmem_limit_bytes=VMEM_BYTES),
        cost_estimate=pl.CostEstimate(
            flops=2 * BLOCK * 1024 * 1536, bytes_accessed=5_000_000, transcendentals=0
        ),
        name="partial_sums",
    )(*a_pieces, *w_pieces)


def mid_body(*refs):
    sums, (resid_ref, hot_ref, mid_ref, send_ref) = refs[:RING], refs[RING:]
    proj = added(*[ref[...] for ref in sums])
    mid = (resid_ref[...].astype(F32) + proj).astype(BF16)
    mid_ref[...] = mid
    send_ref[...] = jnp.dot(hot_ref[...], mid, preferred_element_type=F32).astype(BF16)


def mid_and_slots(sums, resid_cols, hot):
    return pl.pallas_call(
        mid_body,
        in_specs=[pl.BlockSpec(memory_space=pltpu.VMEM)] * (RING + 2),
        out_specs=[pl.BlockSpec(memory_space=pltpu.VMEM)] * 2,
        out_shape=[
            jax.ShapeDtypeStruct((BLOCK, COLS), BF16),
            jax.ShapeDtypeStruct((N_EXP * ROWS, COLS), BF16),
        ],
        compiler_params=pltpu.CompilerParams(vmem_limit_bytes=VMEM_BYTES),
        cost_estimate=pl.CostEstimate(
            flops=2 * BLOCK * N_EXP * ROWS * COLS, bytes_accessed=3_000_000, transcendentals=0
        ),
        name="mid_and_slots",
    )(*sums, resid_cols, hot)


def sum_over_z(parts):
    far, after, ahead, own = parts
    return [own, along_z(far, 2), along_z(after, 1), along_z(ahead, -1)]


def added(*terms):
    total = terms[0].astype(F32)
    for term in terms[1:]:
        total = total + term.astype(F32)
    return total


def norm_body(got_ref, gain_ref, *out_refs):
    for half, out_ref in enumerate(out_refs):
        rows = pl.ds(half * HALF, HALF)
        total = jnp.zeros((HALF, 1), F32)
        for j in range(N_EXP):
            piece = got_ref[j, rows, :].astype(F32)
            total += jnp.sum(piece * piece, axis=1, keepdims=True)
        factor = lax.rsqrt(total * (1.0 / D) + EPS)
        for j in range(N_EXP):
            cols = pl.ds((j % RING * RING + j // RING) * COLS, COLS)
            piece = got_ref[j, rows, :].astype(F32)
            out_ref[:, cols] = (piece * factor * gain_ref[:, cols]).astype(BF16)


def norm_rows(got, mlp_gain):
    return pl.pallas_call(
        norm_body,
        in_specs=[pl.BlockSpec(memory_space=pltpu.VMEM)] * 2,
        out_specs=[pl.BlockSpec(memory_space=pltpu.VMEM)] * 2,
        out_shape=[jax.ShapeDtypeStruct((HALF, D), BF16)] * 2,
        compiler_params=pltpu.CompilerParams(vmem_limit_bytes=VMEM_BYTES),
        cost_estimate=pl.CostEstimate(
            flops=4 * ROWS * D, bytes_accessed=4 * ROWS * D, transcendentals=0
        ),
        name="norm_rows",
    )(got, mlp_gain.reshape(1, D))


STEPS = 6
WIDE = D // STEPS
PIECES = 2 * RING


def hidden_body(*refs):
    x_refs = refs[:PIECES]
    gate_ref, up_ref, out_ref, acc = refs[PIECES:]
    step = pl.program_id(0)
    ff = gate_ref.shape[1]
    rows = jnp.concatenate([r[...] for r in x_refs], axis=0)
    weight = jnp.concatenate([gate_ref[0], up_ref[0]], axis=0)
    part = lax.dot_general(
        rows, weight, (((1,), (1,)), ((), ())), preferred_element_type=F32
    )

    @pl.when(step == 0)
    def _():
        acc[...] = part

    @pl.when(step > 0)
    def _():
        acc[...] += part

    @pl.when(step == STEPS - 1)
    def _():
        out_ref[...] = (jax.nn.silu(acc[:, :ff]) * acc[:, ff:]).astype(BF16)


def hidden_rows(pieces, gate_w, up_w):
    ff = gate_w.shape[1]
    total = PIECES * HALF
    return pl.pallas_call(
        hidden_body,
        grid=(STEPS,),
        in_specs=[pl.BlockSpec((HALF, WIDE), lambda i: (0, i))] * PIECES
        + [pl.BlockSpec((1, ff, WIDE), lambda i: (0, 0, i))] * 2,
        out_specs=pl.BlockSpec((total, ff), lambda i: (0, 0)),
        out_shape=jax.ShapeDtypeStruct((total, ff), BF16),
        scratch_shapes=[pltpu.VMEM((total, 2 * ff), F32)],
        compiler_params=pltpu.CompilerParams(vmem_limit_bytes=VMEM_BYTES),
        cost_estimate=pl.CostEstimate(**LIGHT),
        name="hidden_rows",
    )(*pieces, gate_w, up_w)


def down_rows(hidden, down_w):
    return jnp.dot(hidden, down_w[0], preferred_element_type=F32).astype(BF16)


def both_cores(mine):
    return mine + [other_core(piece) for piece in mine]


def gather_halves(first, second):
    left, right = along_x(first, 1), along_x(first, -1)
    crossed = [other_core(first), other_core(second)]
    second, left, right, crossed = lax.optimization_barrier((second, left, right, crossed))
    far = along_x(left, 1)
    right_2 = along_x(second, -1)
    crossed += [other_core(left), other_core(right)]
    second, far, right_2, crossed = lax.optimization_barrier((second, far, right_2, crossed))
    left_2 = along_x(second, 1)
    far_2 = along_x(right_2, -1)
    far_crossed, right_crossed = lax.optimization_barrier((other_core(far), other_core(right_2)))
    ahead = [first, left, right, far, crossed[0], crossed[2], crossed[3], far_crossed]
    behind = [second, left_2, right_2, far_2]
    behind += [crossed[1], None, right_crossed, None]
    return ahead, behind


def expert_sums(hidden, down_w):
    count = RING * HALF
    theirs = other_core(down_rows(hidden[count:], down_w))
    mine = down_rows(hidden[:count], down_w)
    mine, theirs = lax.optimization_barrier((mine, theirs))
    both = added(mine, theirs).astype(BF16)
    return [both[i * HALF : (i + 1) * HALF] for i in range(RING)]


def to_owners(rows):
    rows = rows.reshape(CAP // 2, N_EXP, D // 128, 128).transpose(1, 0, 2, 3)
    return rows.reshape(N_EXP, CAP // 2 * (D // 128), 128)


def shards(
    q_act,
    k_act,
    v_act,
    log_forget,
    attn_gain,
    w_out,
    resid,
    mlp_gain,
    gate_w,
    up_w,
    down_w,
    expert_ids,
    gate_codes,
):
    tok_dev = resid.shape[0]
    attn_out, chip, arrived = attention(q_act, k_act, v_act, log_forget, attn_gain)
    me_ctx, me_exp, _ = lax.optimization_barrier(
        (lax.axis_index("ctx"), lax.axis_index("exp"), chip)
    )
    me_x, me_core = me_ctx // 2, me_ctx % 2
    me_z, me_y = me_exp // RING, me_exp % RING
    eighth = lax.dynamic_slice_in_dim(w_out, me_ctx * EIGHTH, EIGHTH, 0)
    eighth = eighth.reshape(EIGHTH, N_EXP, COLS).transpose(1, 0, 2)
    block = lambda y, z: lax.dynamic_index_in_dim(
        eighth, (me_y + y) % RING * RING + (me_z + z) % RING, 0, keepdims=False
    )
    eighth = [
        jnp.concatenate([block(y, z) for z in range(RING)], axis=1) for y in range(RING)
    ]
    w_rows = jnp.concatenate(
        [eighth[0], along_y(eighth[1], 1), along_y(eighth[3], -1), along_y(eighth[2], 2)]
    )

    w_rows, arrived = lax.optimization_barrier((w_rows, arrived))
    w_left, w_right = along_x(w_rows, 1), along_x(w_rows, -1)
    steps = jnp.array([0, -1, 1, 2], jnp.int32)
    xs = (me_x + steps) % RING
    order = jnp.concatenate([xs * 2 + me_core, xs * 2 + 1 - me_core])
    col = jnp.arange(BLOCK)
    order = jnp.repeat(order, EIGHTH) * EIGHTH + col % EIGHTH
    shuffle = (col[:, None] == order[None, :]).astype(BF16)
    attn_out = jnp.dot(attn_out, shuffle, preferred_element_type=F32).astype(BF16)

    a_pieces = [attn_out, along_y(attn_out, 1), along_y(attn_out, -1), along_y(attn_out, 2)]

    w_left, w_right, a_pieces[1:3] = lax.optimization_barrier((w_left, w_right, a_pieces[1:3]))
    w_half = w_rows.shape[0] // 2
    w_far = jnp.concatenate([along_x(w_left[:w_half], 1), along_x(w_right[w_half:], -1)])
    near = both_cores([w_rows, w_left, w_right])
    w_far, a_pieces = lax.optimization_barrier((w_far, a_pieces))
    w_pieces = near[:3] + [w_far] + near[3:] + [other_core(w_far)]

    parts = partial_sums(a_pieces, w_pieces)
    resid, expert_ids, _ = lax.optimization_barrier((resid, expert_ids, parts[0]))
    slot = slot_targets(expert_ids)
    blocks = resid.reshape(tok_dev, RING, RING, COLS).transpose(2, 1, 0, 3)
    named = (expert_ids * 8 + slot).T.reshape(1, -1).astype(BF16)
    named = jnp.pad(named, ((0, 7), (0, COLS - named.shape[1])))
    blocks = jnp.concatenate(
        [
            blocks.reshape(N_EXP, tok_dev, COLS),
            jnp.broadcast_to(named[None], (N_EXP,) + named.shape),
        ],
        axis=1,
    )
    blocks = all_to_all_exp(blocks)
    resid_cols = blocks[:, :tok_dev].reshape(N_EXP * tok_dev, COLS)
    named = blocks[:, tok_dev, : 2 * tok_dev].astype(jnp.int32)
    owner = jnp.arange(N_EXP, dtype=jnp.int32)[:, None]
    places = (named // 8 * CAP + named % 8) * N_EXP + owner
    places = places.reshape(N_EXP, 2, tok_dev).transpose(1, 0, 2).reshape(2, N_EXP * tok_dev)
    targets = jnp.arange(N_EXP * ROWS, dtype=jnp.int32)
    targets = (targets // (2 * ROWS)) * ROWS + targets % ROWS
    hot = (targets[:, None] == places[0][None]) | (targets[:, None] == places[1][None])
    hot = hot.astype(BF16)

    proj = sum_over_z(parts)
    mid_cols, send = mid_and_slots(proj, resid_cols, hot)
    got = all_to_all_exp(send.reshape(N_EXP, ROWS, COLS))
    halves = norm_rows(got, mlp_gain)
    ahead, behind = gather_halves(*halves)
    hidden = hidden_rows(ahead, gate_w, up_w)
    hidden, behind[1:4] = lax.optimization_barrier((hidden, behind[1:4]))
    own, left, right, far = expert_sums(hidden, down_w)
    behind[5], behind[7] = other_core(behind[1]), other_core(behind[3])
    behind[0], left, far = lax.optimization_barrier((behind[0], left, far))
    far, left = along_x(far, 1), along_x(left, -1)
    hidden = hidden_rows(behind, gate_w, up_w)
    hidden, far, left = lax.optimization_barrier((hidden, far, left))
    right = along_x(added(right, far).astype(BF16), 1)
    own_2, left_2, right_2, far_2 = expert_sums(hidden, down_w)
    part = HALF // 2
    up, down = along_x(far_2[:part], 1), along_x(far_2[part:], -1)
    lane_rows = D // 128
    sent = jnp.concatenate(
        [
            to_owners(added(own, left, right).astype(BF16)),
            mid_cols.reshape(N_EXP, tok_dev * COLS // 128, 128),
        ],
        axis=1,
    )
    returned = [all_to_all_exp(sent)]
    right_2 = jnp.concatenate([added(right_2[:part], up).astype(BF16), right_2[part:]])
    left_2 = jnp.concatenate([left_2[:part], added(left_2[part:], down).astype(BF16)])
    from_left, from_right = along_x(right_2, 1), along_x(left_2, -1)
    back = to_owners(added(own_2, from_left, from_right).astype(BF16))
    returned.append(all_to_all_exp(back))
    mid_own = returned[0][:, CAP // 2 * lane_rows :]
    returned[0] = returned[0][:, : CAP // 2 * lane_rows]
    returned = [
        part.reshape(EXPERTS, 2, CAP // 2, lane_rows, 128).astype(F32) for part in returned
    ]
    outputs = jnp.concatenate([jnp.sum(part, axis=1) for part in returned], axis=1)
    outputs = outputs.reshape(EXPERTS * CAP, D)

    own_place = (expert_ids * CAP + slot)[:, :, None]
    route = gate_codes.astype(F32)
    route = route / jnp.sum(route, axis=1, keepdims=True)
    slots = jnp.arange(EXPERTS * CAP, dtype=jnp.int32)[None, None, :]
    combine = jnp.sum(jnp.where(own_place == slots, route[:, :, None], 0.0), axis=1)
    moe = jnp.dot(combine, outputs, precision=lax.Precision.HIGHEST, preferred_element_type=F32)
    mid_f = mid_own.reshape(RING, RING, tok_dev, COLS).transpose(2, 1, 0, 3)
    mid_f = mid_f.reshape(tok_dev, D).astype(F32)
    return (mid_f + moe).astype(BF16)


def solution(mesh):
    placed = (
        P("ctx", "exp"),
        P("ctx", "exp"),
        P("ctx", "exp"),
        P("exp", "ctx"),
        P("exp"),
        P("exp", None),
        P(("ctx", "exp"), None),
        P(),
        P("exp", "ctx", None),
        P("exp", "ctx", None),
        P("exp", "ctx", None),
        P(("ctx", "exp"), None),
        P(("ctx", "exp"), None),
    )
    return jax.shard_map(
        shards, mesh=mesh, in_specs=placed, out_specs=P(("ctx", "exp"), None), check_vma=False
    )
```

```python
import jax
import jax.numpy as jnp
from jax import lax
from jax.experimental import pallas as pl
from jax.experimental.pallas import tpu as pltpu
from jax.sharding import PartitionSpec as P

D = 6144
HEAD_DIM = 128
EXPERTS = 8
BLOCK = 256
N_CTX = 8
N_EXP = 16
RING = 4
CAP = 6
ROWS = N_EXP * CAP
HALF = ROWS // 2
COLS = D // N_EXP
EIGHTH = 256 // N_CTX
EPS = 1e-06
F32 = jnp.float32
BF16 = jnp.bfloat16
VMEM_BYTES = 24 * 1024 * 1024
LIGHT = dict(flops=1000, bytes_accessed=1000, transcendentals=0)


def along_x(value, steps):
    pairs = [(c, ((c // 2 + steps) % RING) * 2 + c % 2) for c in range(N_CTX)]
    return lax.ppermute(value, "ctx", pairs)


def other_core(value):
    return lax.ppermute(value, "ctx", [(c, c ^ 1) for c in range(N_CTX)])


def along_y(value, steps):
    pairs = [(j, j // RING * RING + (j % RING + steps) % RING) for j in range(N_EXP)]
    return lax.ppermute(value, "exp", pairs)


def along_z(value, steps):
    pairs = [(j, (j + RING * steps) % N_EXP) for j in range(N_EXP)]
    return lax.ppermute(value, "exp", pairs)


def next_chips(value, steps):
    pairs = [(c, c + 2 * steps) for c in range(N_CTX - 2 * steps)]
    return lax.ppermute(value, "ctx", pairs)


def all_to_all_exp(value):
    return lax.all_to_all(value, "exp", split_axis=0, concat_axis=0, tiled=True)


HEADS = 2
STATE = HEADS * HEAD_DIM
PACKED = STATE + 16
EXACT = dict(precision=lax.Precision.HIGHEST, preferred_element_type=F32)


def store_packed(out_ref, states, logs):
    for h in range(HEADS):
        out_ref[h * HEAD_DIM : (h + 1) * HEAD_DIM, :] = states[h].astype(BF16)
    log = jnp.concatenate([jnp.broadcast_to(x, (1, HEAD_DIM)) for x in logs], axis=0)
    a = log.astype(BF16).astype(F32)
    b = (log - a).astype(BF16).astype(F32)
    c = (log - a - b).astype(BF16).astype(F32)
    rest = jnp.zeros((16 - 3 * HEADS, HEAD_DIM), F32)
    out_ref[STATE:, :] = jnp.concatenate([a, b, c, rest], axis=0).astype(BF16)


def load_packed(ref):
    rows = ref[STATE:, :].astype(F32)
    states = [ref[h * HEAD_DIM : (h + 1) * HEAD_DIM, :].astype(F32) for h in range(HEADS)]
    logs = [rows[h : h + 1] + rows[h + 2 : h + 3] + rows[h + 4 : h + 5] for h in range(HEADS)]
    return states, logs


def state_body(k_ref, v_ref, rate_ref, packed_ref, update_ref, row_ref, col_ref):
    count = k_ref.shape[0]
    at = lax.broadcasted_iota(jnp.int32, (count, count), 0)
    upto = lax.broadcasted_iota(jnp.int32, (count, count), 1)
    lower = (at >= upto).astype(F32)
    rates = jnp.concatenate([rate_ref[...], jnp.zeros((8 - HEADS, count), F32)], axis=0)
    dims = (((1,), (1,)), ((), ()))
    row = lax.dot_general(rates, lower, dims, **EXACT)
    col = lax.dot_general(lower, rates, dims, **EXACT)
    row_ref[...] = row
    col_ref[...] = col
    updates, ends = [], []
    for h in range(HEADS):
        lanes = pl.ds(h * HEAD_DIM, HEAD_DIM)
        end = row[h : h + 1, count - 1 : count]
        faded = k_ref[:, lanes].astype(F32) * jnp.exp(end - col[:, h : h + 1])
        update = lax.dot_general(
            faded, v_ref[:, lanes].astype(F32), (((0,), (0,)), ((), ())), **EXACT
        )
        update_ref[h * HEAD_DIM : (h + 1) * HEAD_DIM, :] = update
        updates.append(update)
        ends.append(end)
    store_packed(packed_ref, updates, ends)


def chip_body(core_ref, mate_ref, update_ref, row_ref, out_ref):
    second = core_ref[0] == 1
    mates, mate_logs = load_packed(mate_ref)
    states, logs = [], []
    count = row_ref.shape[1]
    for h in range(HEADS):
        own = update_ref[h * HEAD_DIM : (h + 1) * HEAD_DIM, :]
        end = jnp.broadcast_to(row_ref[h : h + 1, count - 1 : count], (1, HEAD_DIM))
        after = jnp.exp(end) * mates[h] + own
        before = jnp.exp(mate_logs[h]) * own + mates[h]
        states.append(jnp.where(second, after, before))
        logs.append(end + mate_logs[h])
    store_packed(out_ref, states, logs)


def heads_body(place_ref, q_ref, k_ref, v_ref, row_ref, col_ref, gain_ref, *refs):
    mate_ref, arrived, out_ref = refs[0], refs[1:-1], refs[-1]
    count = q_ref.shape[0]
    scale = HEAD_DIM ** (-0.5)
    second = place_ref[1] == 1
    mates, mate_logs = load_packed(mate_ref)
    incoming = [jnp.zeros((HEAD_DIM, HEAD_DIM), F32)] * HEADS
    passed = [jnp.zeros((1, HEAD_DIM), F32)] * HEADS
    for ref in arrived:
        states, logs = load_packed(ref)
        for h in range(HEADS):
            incoming[h] = incoming[h] + jnp.exp(passed[h]) * states[h]
            passed[h] = passed[h] + logs[h]
    at = lax.broadcasted_iota(jnp.int32, (count, count), 0)
    upto = lax.broadcasted_iota(jnp.int32, (count, count), 1)
    causal = at >= upto
    outs = []
    for h in range(HEADS):
        lanes = pl.ds(h * HEAD_DIM, HEAD_DIM)
        state = jnp.where(second, jnp.exp(mate_logs[h]) * incoming[h] + mates[h], incoming[h])
        query, value = q_ref[:, lanes], v_ref[:, lanes]
        col = col_ref[:, h : h + 1]
        differ = jnp.where(causal, col - row_ref[h : h + 1, :], 0.0)
        decay = jnp.where(causal, jnp.exp(differ), 0.0)
        scores = lax.dot_general(
            query, k_ref[:, lanes], (((1,), (1,)), ((), ())), preferred_element_type=F32
        )
        scores = (scores * scale * decay).astype(BF16)
        intra = jnp.dot(scores, value, preferred_element_type=F32)
        inter = jnp.dot(query.astype(F32), state, **EXACT)
        out = intra + scale * jnp.exp(col) * inter
        meansq = jnp.mean(out * out, axis=1, keepdims=True)
        outs.append((out * lax.rsqrt(meansq + EPS) * gain_ref[:, lanes]).astype(BF16))
    piece = upto // EIGHTH
    turn = piece % RING
    step = jnp.where(turn == 1, RING - 1, jnp.where(turn == 2, 1, jnp.where(turn == 3, 2, 0)))
    x = (place_ref[0] + step) % RING
    core = jnp.where(piece >= RING, 1 - place_ref[1], place_ref[1])
    wanted = (x * 2 + core) * EIGHTH + upto % EIGHTH
    shuffle = (at == wanted).astype(F32).astype(BF16)
    out_ref[...] = jnp.dot(
        jnp.concatenate(outs, axis=1), shuffle, preferred_element_type=F32
    ).astype(BF16)


def attention(q_act, k_act, v_act, log_forget, attn_gain):
    rows = q_act.shape[0]
    vmem = pl.BlockSpec(memory_space=pltpu.VMEM)
    smem = pl.BlockSpec(memory_space=pltpu.SMEM)
    params = pltpu.CompilerParams(vmem_limit_bytes=VMEM_BYTES)
    packed_type = jax.ShapeDtypeStruct((PACKED, HEAD_DIM), BF16)
    me = lax.axis_index("ctx")
    place = jnp.stack([me // 2, me % 2]).astype(jnp.int32)
    own, update, row, col = pl.pallas_call(
        state_body,
        in_specs=[vmem] * 3,
        out_specs=[vmem] * 4,
        out_shape=[
            packed_type,
            jax.ShapeDtypeStruct((STATE, HEAD_DIM), F32),
            jax.ShapeDtypeStruct((8, rows), F32),
            jax.ShapeDtypeStruct((rows, 8), F32),
        ],
        compiler_params=params,
        cost_estimate=pl.CostEstimate(**LIGHT),
        name="state",
    )(k_act, v_act, log_forget)
    mate = other_core(own)
    chip = pl.pallas_call(
        chip_body,
        in_specs=[smem] + [vmem] * 3,
        out_specs=vmem,
        out_shape=packed_type,
        compiler_params=params,
        cost_estimate=pl.CostEstimate(**LIGHT),
        name="chip_state",
    )(place[1:], mate, update, row)
    arrived = [next_chips(chip, steps) for steps in range(1, RING)]
    attn_out = pl.pallas_call(
        heads_body,
        in_specs=[smem] + [vmem] * (7 + len(arrived)),
        out_specs=vmem,
        out_shape=jax.ShapeDtypeStruct((rows, STATE), BF16),
        compiler_params=params,
        cost_estimate=pl.CostEstimate(**LIGHT),
        name="heads",
    )(place, q_act, k_act, v_act, row, col, attn_gain.reshape(1, -1), mate, *arrived)
    return attn_out, chip, arrived


def slot_targets(ids):
    flat = ids.reshape(-1)
    onehot = (flat[:, None] == jnp.arange(EXPERTS, dtype=jnp.int32)[None, :]).astype(jnp.int32)
    before = jnp.cumsum(onehot, axis=0) - onehot
    slot = jnp.sum(before * onehot, axis=1)
    return slot.reshape(ids.shape)


def partial_body(*refs):
    a_refs, w_refs = refs[:RING], refs[RING : RING + N_CTX]
    out_refs = refs[RING + N_CTX :]
    for out_ref, k in zip(out_refs, (2, 1, 3, 0)):
        cols = pl.ds(k * COLS, COLS)
        total = None
        for d, a_ref in enumerate(a_refs):
            rows = pl.ds(d * EIGHTH, EIGHTH)
            weight = jnp.concatenate([w_ref[rows, cols] for w_ref in w_refs], axis=0)
            part = jnp.dot(a_ref[...], weight, preferred_element_type=F32)
            total = part if total is None else total + part
        out_ref[...] = total.astype(BF16)


def partial_sums(a_pieces, w_pieces):
    return pl.pallas_call(
        partial_body,
        in_specs=[pl.BlockSpec(memory_space=pltpu.VMEM)] * (RING + N_CTX),
        out_specs=[pl.BlockSpec(memory_space=pltpu.VMEM)] * RING,
        out_shape=[jax.ShapeDtypeStruct((BLOCK, COLS), BF16)] * RING,
        compiler_params=pltpu.CompilerParams(vmem_limit_bytes=VMEM_BYTES),
        cost_estimate=pl.CostEstimate(
            flops=2 * BLOCK * 1024 * 1536, bytes_accessed=5_000_000, transcendentals=0
        ),
        name="partial_sums",
    )(*a_pieces, *w_pieces)


def mid_body(*refs):
    sums, (resid_ref, hot_ref, mid_ref, send_ref) = refs[:RING], refs[RING:]
    proj = added(*[ref[...] for ref in sums])
    mid = (resid_ref[...].astype(F32) + proj).astype(BF16)
    mid_ref[...] = mid
    send_ref[...] = jnp.dot(hot_ref[...], mid, preferred_element_type=F32).astype(BF16)


def mid_and_slots(sums, resid_cols, hot):
    return pl.pallas_call(
        mid_body,
        in_specs=[pl.BlockSpec(memory_space=pltpu.VMEM)] * (RING + 2),
        out_specs=[pl.BlockSpec(memory_space=pltpu.VMEM)] * 2,
        out_shape=[
            jax.ShapeDtypeStruct((BLOCK, COLS), BF16),
            jax.ShapeDtypeStruct((N_EXP * ROWS, COLS), BF16),
        ],
        compiler_params=pltpu.CompilerParams(vmem_limit_bytes=VMEM_BYTES),
        cost_estimate=pl.CostEstimate(
            flops=2 * BLOCK * N_EXP * ROWS * COLS, bytes_accessed=3_000_000, transcendentals=0
        ),
        name="mid_and_slots",
    )(*sums, resid_cols, hot)


def sum_over_z(parts):
    far, after, ahead, own = parts
    return [own, along_z(far, 2), along_z(after, 1), along_z(ahead, -1)]


def added(*terms):
    total = terms[0].astype(F32)
    for term in terms[1:]:
        total = total + term.astype(F32)
    return total


def norm_body(got_ref, gain_ref, *out_refs):
    for half, out_ref in enumerate(out_refs):
        rows = pl.ds(half * HALF, HALF)
        total = jnp.zeros((HALF, 1), F32)
        for j in range(N_EXP):
            piece = got_ref[j, rows, :].astype(F32)
            total += jnp.sum(piece * piece, axis=1, keepdims=True)
        factor = lax.rsqrt(total * (1.0 / D) + EPS)
        for j in range(N_EXP):
            cols = pl.ds((j % RING * RING + j // RING) * COLS, COLS)
            piece = got_ref[j, rows, :].astype(F32)
            out_ref[:, cols] = (piece * factor * gain_ref[:, cols]).astype(BF16)


def norm_rows(got, mlp_gain):
    return pl.pallas_call(
        norm_body,
        in_specs=[pl.BlockSpec(memory_space=pltpu.VMEM)] * 2,
        out_specs=[pl.BlockSpec(memory_space=pltpu.VMEM)] * 2,
        out_shape=[jax.ShapeDtypeStruct((HALF, D), BF16)] * 2,
        compiler_params=pltpu.CompilerParams(vmem_limit_bytes=VMEM_BYTES),
        cost_estimate=pl.CostEstimate(
            flops=4 * ROWS * D, bytes_accessed=4 * ROWS * D, transcendentals=0
        ),
        name="norm_rows",
    )(got, mlp_gain.reshape(1, D))


STEPS = 6
WIDE = D // STEPS
PIECES = 2 * RING


def hidden_body(*refs):
    x_refs = refs[:PIECES]
    gate_ref, up_ref, out_ref, acc = refs[PIECES:]
    step = pl.program_id(0)
    ff = gate_ref.shape[1]
    rows = jnp.concatenate([r[...] for r in x_refs], axis=0)
    weight = jnp.concatenate([gate_ref[0], up_ref[0]], axis=0)
    part = lax.dot_general(
        rows, weight, (((1,), (1,)), ((), ())), preferred_element_type=F32
    )

    @pl.when(step == 0)
    def _():
        acc[...] = part

    @pl.when(step > 0)
    def _():
        acc[...] += part

    @pl.when(step == STEPS - 1)
    def _():
        out_ref[...] = (jax.nn.silu(acc[:, :ff]) * acc[:, ff:]).astype(BF16)


def hidden_rows(pieces, gate_w, up_w):
    ff = gate_w.shape[1]
    total = PIECES * HALF
    return pl.pallas_call(
        hidden_body,
        grid=(STEPS,),
        in_specs=[pl.BlockSpec((HALF, WIDE), lambda i: (0, i))] * PIECES
        + [pl.BlockSpec((1, ff, WIDE), lambda i: (0, 0, i))] * 2,
        out_specs=pl.BlockSpec((total, ff), lambda i: (0, 0)),
        out_shape=jax.ShapeDtypeStruct((total, ff), BF16),
        scratch_shapes=[pltpu.VMEM((total, 2 * ff), F32)],
        compiler_params=pltpu.CompilerParams(vmem_limit_bytes=VMEM_BYTES),
        cost_estimate=pl.CostEstimate(**LIGHT),
        name="hidden_rows",
    )(*pieces, gate_w, up_w)


def down_rows(hidden, down_w):
    return jnp.dot(hidden, down_w[0], preferred_element_type=F32).astype(BF16)


def both_cores(mine):
    return mine + [other_core(piece) for piece in mine]


def gather_halves(first, second):
    left, right = along_x(first, 1), along_x(first, -1)
    crossed = [other_core(first), other_core(second)]
    second, left, right, crossed = lax.optimization_barrier((second, left, right, crossed))
    far = along_x(left, 1)
    right_2 = along_x(second, -1)
    crossed += [other_core(left), other_core(right)]
    second, far, right_2, crossed = lax.optimization_barrier((second, far, right_2, crossed))
    left_2 = along_x(second, 1)
    far_2 = along_x(right_2, -1)
    far_crossed, right_crossed = lax.optimization_barrier((other_core(far), other_core(right_2)))
    ahead = [first, left, right, far, crossed[0], crossed[2], crossed[3], far_crossed]
    behind = [second, left_2, right_2, far_2]
    behind += [crossed[1], None, right_crossed, None]
    return ahead, behind


def expert_sums(hidden, down_w):
    count = RING * HALF
    theirs = other_core(down_rows(hidden[count:], down_w))
    mine = down_rows(hidden[:count], down_w)
    mine, theirs = lax.optimization_barrier((mine, theirs))
    both = added(mine, theirs).astype(BF16)
    return [both[i * HALF : (i + 1) * HALF] for i in range(RING)]


def to_owners(rows):
    rows = rows.reshape(CAP // 2, N_EXP, D // 128, 128).transpose(1, 0, 2, 3)
    return rows.reshape(N_EXP, CAP // 2 * (D // 128), 128)


def shards(
    q_act,
    k_act,
    v_act,
    log_forget,
    attn_gain,
    w_out,
    resid,
    mlp_gain,
    gate_w,
    up_w,
    down_w,
    expert_ids,
    gate_codes,
):
    tok_dev = resid.shape[0]
    attn_out, chip, arrived = attention(q_act, k_act, v_act, log_forget, attn_gain)
    me_ctx, me_exp, _ = lax.optimization_barrier(
        (lax.axis_index("ctx"), lax.axis_index("exp"), chip)
    )
    me_z, me_y = me_exp // RING, me_exp % RING
    eighth = lax.dynamic_slice_in_dim(w_out, me_ctx * EIGHTH, EIGHTH, 0)
    eighth = eighth.reshape(EIGHTH, N_EXP, COLS).transpose(1, 0, 2)
    block = lambda y, z: lax.dynamic_index_in_dim(
        eighth, (me_y + y) % RING * RING + (me_z + z) % RING, 0, keepdims=False
    )
    eighth = [
        jnp.concatenate([block(y, z) for z in range(RING)], axis=1) for y in range(RING)
    ]
    w_rows = jnp.concatenate(
        [eighth[0], along_y(eighth[1], 1), along_y(eighth[3], -1), along_y(eighth[2], 2)]
    )

    w_rows, arrived = lax.optimization_barrier((w_rows, arrived))
    w_left, w_right = along_x(w_rows, 1), along_x(w_rows, -1)
    a_pieces = [attn_out, along_y(attn_out, 1), along_y(attn_out, -1), along_y(attn_out, 2)]

    w_left, w_right, a_pieces[1:3] = lax.optimization_barrier((w_left, w_right, a_pieces[1:3]))
    w_half = w_rows.shape[0] // 2
    w_far = jnp.concatenate([along_x(w_left[:w_half], 1), along_x(w_right[w_half:], -1)])
    near = both_cores([w_rows, w_left, w_right])
    w_far, a_pieces = lax.optimization_barrier((w_far, a_pieces))
    w_pieces = near[:3] + [w_far] + near[3:] + [other_core(w_far)]

    parts = partial_sums(a_pieces, w_pieces)
    resid, expert_ids, _ = lax.optimization_barrier((resid, expert_ids, parts[0]))
    slot = slot_targets(expert_ids)
    blocks = resid.reshape(tok_dev, RING, RING, COLS).transpose(2, 1, 0, 3)
    named = (expert_ids * 8 + slot).T.reshape(1, -1).astype(BF16)
    named = jnp.pad(named, ((0, 7), (0, COLS - named.shape[1])))
    blocks = jnp.concatenate(
        [
            blocks.reshape(N_EXP, tok_dev, COLS),
            jnp.broadcast_to(named[None], (N_EXP,) + named.shape),
        ],
        axis=1,
    )
    blocks = all_to_all_exp(blocks)
    resid_cols = blocks[:, :tok_dev].reshape(N_EXP * tok_dev, COLS)
    named = blocks[:, tok_dev, : 2 * tok_dev].astype(jnp.int32)
    owner = jnp.arange(N_EXP, dtype=jnp.int32)[:, None]
    places = (named // 8 * CAP + named % 8) * N_EXP + owner
    places = places.reshape(N_EXP, 2, tok_dev).transpose(1, 0, 2).reshape(2, N_EXP * tok_dev)
    targets = jnp.arange(N_EXP * ROWS, dtype=jnp.int32)
    targets = (targets // (2 * ROWS)) * ROWS + targets % ROWS
    hot = (targets[:, None] == places[0][None]) | (targets[:, None] == places[1][None])
    hot = hot.astype(BF16)

    proj = sum_over_z(parts)
    mid_cols, send = mid_and_slots(proj, resid_cols, hot)
    got = all_to_all_exp(send.reshape(N_EXP, ROWS, COLS))
    halves = norm_rows(got, mlp_gain)
    ahead, behind = gather_halves(*halves)
    hidden = hidden_rows(ahead, gate_w, up_w)
    hidden, behind[1:4] = lax.optimization_barrier((hidden, behind[1:4]))
    own, left, right, far = expert_sums(hidden, down_w)
    behind[5], behind[7] = other_core(behind[1]), other_core(behind[3])
    behind[0], left, far = lax.optimization_barrier((behind[0], left, far))
    far, left = along_x(far, 1), along_x(left, -1)
    hidden = hidden_rows(behind, gate_w, up_w)
    hidden, far, left = lax.optimization_barrier((hidden, far, left))
    right = along_x(added(right, far).astype(BF16), 1)
    own_2, left_2, right_2, far_2 = expert_sums(hidden, down_w)
    part = HALF // 2
    up, down = along_x(far_2[:part], 1), along_x(far_2[part:], -1)
    lane_rows = D // 128
    sent = jnp.concatenate(
        [
            to_owners(added(own, left, right).astype(BF16)),
            mid_cols.reshape(N_EXP, tok_dev * COLS // 128, 128),
        ],
        axis=1,
    )
    returned = [all_to_all_exp(sent)]
    right_2 = jnp.concatenate([added(right_2[:part], up).astype(BF16), right_2[part:]])
    left_2 = jnp.concatenate([left_2[:part], added(left_2[part:], down).astype(BF16)])
    from_left, from_right = along_x(right_2, 1), along_x(left_2, -1)
    back = to_owners(added(own_2, from_left, from_right).astype(BF16))
    returned.append(all_to_all_exp(back))
    mid_own = returned[0][:, CAP // 2 * lane_rows :]
    returned[0] = returned[0][:, : CAP // 2 * lane_rows]
    returned = [
        part.reshape(EXPERTS, 2, CAP // 2, lane_rows, 128).astype(F32) for part in returned
    ]
    outputs = jnp.concatenate([jnp.sum(part, axis=1) for part in returned], axis=1)
    outputs = outputs.reshape(EXPERTS * CAP, D)

    own_place = (expert_ids * CAP + slot)[:, :, None]
    route = gate_codes.astype(F32)
    route = route / jnp.sum(route, axis=1, keepdims=True)
    slots = jnp.arange(EXPERTS * CAP, dtype=jnp.int32)[None, None, :]
    combine = jnp.sum(jnp.where(own_place == slots, route[:, :, None], 0.0), axis=1)
    moe = jnp.dot(combine, outputs, precision=lax.Precision.HIGHEST, preferred_element_type=F32)
    mid_f = mid_own.reshape(RING, RING, tok_dev, COLS).transpose(2, 1, 0, 3)
    mid_f = mid_f.reshape(tok_dev, D).astype(F32)
    return (mid_f + moe).astype(BF16)


def solution(mesh):
    placed = (
        P("ctx", "exp"),
        P("ctx", "exp"),
        P("ctx", "exp"),
        P("exp", "ctx"),
        P("exp"),
        P("exp", None),
        P(("ctx", "exp"), None),
        P(),
        P("exp", "ctx", None),
        P("exp", "ctx", None),
        P("exp", "ctx", None),
        P(("ctx", "exp"), None),
        P(("ctx", "exp"), None),
    )
    return jax.shard_map(
        shards, mesh=mesh, in_specs=placed, out_specs=P(("ctx", "exp"), None), check_vma=False
    )
```

```python
import jax
import jax.numpy as jnp
from jax import lax
from jax.experimental import pallas as pl
from jax.experimental.pallas import tpu as pltpu
from jax.sharding import PartitionSpec as P

D = 6144
HEAD_DIM = 128
EXPERTS = 8
BLOCK = 256
N_CTX = 8
N_EXP = 16
RING = 4
CAP = 6
ROWS = N_EXP * CAP
HALF = ROWS // 2
COLS = D // N_EXP
EIGHTH = 256 // N_CTX
EPS = 1e-06
F32 = jnp.float32
BF16 = jnp.bfloat16
VMEM_BYTES = 24 * 1024 * 1024
LIGHT = dict(flops=1000, bytes_accessed=1000, transcendentals=0)


def along_x(value, steps):
    pairs = [(c, ((c // 2 + steps) % RING) * 2 + c % 2) for c in range(N_CTX)]
    return lax.ppermute(value, "ctx", pairs)


def other_core(value):
    return lax.ppermute(value, "ctx", [(c, c ^ 1) for c in range(N_CTX)])


def along_y(value, steps):
    pairs = [(j, j // RING * RING + (j % RING + steps) % RING) for j in range(N_EXP)]
    return lax.ppermute(value, "exp", pairs)


def along_z(value, steps):
    pairs = [(j, (j + RING * steps) % N_EXP) for j in range(N_EXP)]
    return lax.ppermute(value, "exp", pairs)


def next_chips(value, steps):
    pairs = [(c, c + 2 * steps) for c in range(N_CTX - 2 * steps)]
    return lax.ppermute(value, "ctx", pairs)


def all_to_all_exp(value):
    return lax.all_to_all(value, "exp", split_axis=0, concat_axis=0, tiled=True)


HEADS = 2
STATE = HEADS * HEAD_DIM
PACKED = STATE + 16
EXACT = dict(precision=lax.Precision.HIGHEST, preferred_element_type=F32)


def store_packed(out_ref, states, logs):
    for h in range(HEADS):
        out_ref[h * HEAD_DIM : (h + 1) * HEAD_DIM, :] = states[h].astype(BF16)
    log = jnp.concatenate([jnp.broadcast_to(x, (1, HEAD_DIM)) for x in logs], axis=0)
    a = log.astype(BF16).astype(F32)
    b = (log - a).astype(BF16).astype(F32)
    c = (log - a - b).astype(BF16).astype(F32)
    rest = jnp.zeros((16 - 3 * HEADS, HEAD_DIM), F32)
    out_ref[STATE:, :] = jnp.concatenate([a, b, c, rest], axis=0).astype(BF16)


def load_packed(ref):
    rows = ref[STATE:, :].astype(F32)
    states = [ref[h * HEAD_DIM : (h + 1) * HEAD_DIM, :].astype(F32) for h in range(HEADS)]
    logs = [rows[h : h + 1] + rows[h + 2 : h + 3] + rows[h + 4 : h + 5] for h in range(HEADS)]
    return states, logs


def state_body(k_ref, v_ref, rate_ref, packed_ref, update_ref, row_ref, col_ref):
    count = k_ref.shape[0]
    at = lax.broadcasted_iota(jnp.int32, (count, count), 0)
    upto = lax.broadcasted_iota(jnp.int32, (count, count), 1)
    lower = (at >= upto).astype(F32)
    rates = jnp.concatenate([rate_ref[...], jnp.zeros((8 - HEADS, count), F32)], axis=0)
    dims = (((1,), (1,)), ((), ()))
    row = lax.dot_general(rates, lower, dims, **EXACT)
    col = lax.dot_general(lower, rates, dims, **EXACT)
    row_ref[...] = row
    col_ref[...] = col
    updates, ends = [], []
    for h in range(HEADS):
        lanes = pl.ds(h * HEAD_DIM, HEAD_DIM)
        end = row[h : h + 1, count - 1 : count]
        faded = k_ref[:, lanes].astype(F32) * jnp.exp(end - col[:, h : h + 1])
        update = lax.dot_general(
            faded, v_ref[:, lanes].astype(F32), (((0,), (0,)), ((), ())), **EXACT
        )
        update_ref[h * HEAD_DIM : (h + 1) * HEAD_DIM, :] = update
        updates.append(update)
        ends.append(end)
    store_packed(packed_ref, updates, ends)


def chip_body(core_ref, mate_ref, update_ref, row_ref, out_ref):
    second = core_ref[0] == 1
    mates, mate_logs = load_packed(mate_ref)
    states, logs = [], []
    count = row_ref.shape[1]
    for h in range(HEADS):
        own = update_ref[h * HEAD_DIM : (h + 1) * HEAD_DIM, :]
        end = jnp.broadcast_to(row_ref[h : h + 1, count - 1 : count], (1, HEAD_DIM))
        after = jnp.exp(end) * mates[h] + own
        before = jnp.exp(mate_logs[h]) * own + mates[h]
        states.append(jnp.where(second, after, before))
        logs.append(end + mate_logs[h])
    store_packed(out_ref, states, logs)


def heads_body(place_ref, q_ref, k_ref, v_ref, row_ref, col_ref, gain_ref, *refs):
    mate_ref, arrived, out_ref = refs[0], refs[1:-1], refs[-1]
    count = q_ref.shape[0]
    scale = HEAD_DIM ** (-0.5)
    second = place_ref[1] == 1
    mates, mate_logs = load_packed(mate_ref)
    incoming = [jnp.zeros((HEAD_DIM, HEAD_DIM), F32)] * HEADS
    passed = [jnp.zeros((1, HEAD_DIM), F32)] * HEADS
    for ref in arrived:
        states, logs = load_packed(ref)
        for h in range(HEADS):
            incoming[h] = incoming[h] + jnp.exp(passed[h]) * states[h]
            passed[h] = passed[h] + logs[h]
    at = lax.broadcasted_iota(jnp.int32, (count, count), 0)
    upto = lax.broadcasted_iota(jnp.int32, (count, count), 1)
    causal = at >= upto
    outs = []
    for h in range(HEADS):
        lanes = pl.ds(h * HEAD_DIM, HEAD_DIM)
        state = jnp.where(second, jnp.exp(mate_logs[h]) * incoming[h] + mates[h], incoming[h])
        query, value = q_ref[:, lanes], v_ref[:, lanes]
        col = col_ref[:, h : h + 1]
        differ = jnp.where(causal, col - row_ref[h : h + 1, :], 0.0)
        decay = jnp.where(causal, jnp.exp(differ), 0.0)
        scores = lax.dot_general(
            query, k_ref[:, lanes], (((1,), (1,)), ((), ())), preferred_element_type=F32
        )
        scores = (scores * scale * decay).astype(BF16)
        intra = jnp.dot(scores, value, preferred_element_type=F32)
        inter = jnp.dot(query.astype(F32), state, **EXACT)
        out = intra + scale * jnp.exp(col) * inter
        meansq = jnp.mean(out * out, axis=1, keepdims=True)
        outs.append((out * lax.rsqrt(meansq + EPS) * gain_ref[:, lanes]).astype(BF16))
    piece = upto // EIGHTH
    turn = piece % RING
    step = jnp.where(turn == 1, RING - 1, jnp.where(turn == 2, 1, jnp.where(turn == 3, 2, 0)))
    x = (place_ref[0] + step) % RING
    core = jnp.where(piece >= RING, 1 - place_ref[1], place_ref[1])
    wanted = (x * 2 + core) * EIGHTH + upto % EIGHTH
    shuffle = (at == wanted).astype(F32).astype(BF16)
    out_ref[...] = jnp.dot(
        jnp.concatenate(outs, axis=1), shuffle, preferred_element_type=F32
    ).astype(BF16)


def attention(q_act, k_act, v_act, log_forget, attn_gain):
    rows = q_act.shape[0]
    vmem = pl.BlockSpec(memory_space=pltpu.VMEM)
    smem = pl.BlockSpec(memory_space=pltpu.SMEM)
    params = pltpu.CompilerParams(vmem_limit_bytes=VMEM_BYTES)
    packed_type = jax.ShapeDtypeStruct((PACKED, HEAD_DIM), BF16)
    me = lax.axis_index("ctx")
    place = jnp.stack([me // 2, me % 2]).astype(jnp.int32)
    own, update, row, col = pl.pallas_call(
        state_body,
        in_specs=[vmem] * 3,
        out_specs=[vmem] * 4,
        out_shape=[
            packed_type,
            jax.ShapeDtypeStruct((STATE, HEAD_DIM), F32),
            jax.ShapeDtypeStruct((8, rows), F32),
            jax.ShapeDtypeStruct((rows, 8), F32),
        ],
        compiler_params=params,
        cost_estimate=pl.CostEstimate(**LIGHT),
        name="state",
    )(k_act, v_act, log_forget)
    mate = other_core(own)
    chip = pl.pallas_call(
        chip_body,
        in_specs=[smem] + [vmem] * 3,
        out_specs=vmem,
        out_shape=packed_type,
        compiler_params=params,
        cost_estimate=pl.CostEstimate(**LIGHT),
        name="chip_state",
    )(place[1:], mate, update, row)
    arrived = [next_chips(chip, steps) for steps in range(1, RING)]
    attn_out = pl.pallas_call(
        heads_body,
        in_specs=[smem] + [vmem] * (7 + len(arrived)),
        out_specs=vmem,
        out_shape=jax.ShapeDtypeStruct((rows, STATE), BF16),
        compiler_params=params,
        cost_estimate=pl.CostEstimate(**LIGHT),
        name="heads",
    )(place, q_act, k_act, v_act, row, col, attn_gain.reshape(1, -1), mate, *arrived)
    return attn_out, chip, arrived


def slot_targets(ids):
    flat = ids.reshape(-1)
    onehot = (flat[:, None] == jnp.arange(EXPERTS, dtype=jnp.int32)[None, :]).astype(jnp.int32)
    before = jnp.cumsum(onehot, axis=0) - onehot
    slot = jnp.sum(before * onehot, axis=1)
    return slot.reshape(ids.shape)


def partial_body(*refs):
    a_refs, w_refs = refs[:RING], refs[RING : RING + N_CTX]
    out_refs = refs[RING + N_CTX :]
    for out_ref, k in zip(out_refs, (2, 1, 3, 0)):
        cols = pl.ds(k * COLS, COLS)
        total = None
        for d, a_ref in enumerate(a_refs):
            rows = pl.ds(d * EIGHTH, EIGHTH)
            weight = jnp.concatenate([w_ref[rows, cols] for w_ref in w_refs], axis=0)
            part = jnp.dot(a_ref[...], weight, preferred_element_type=F32)
            total = part if total is None else total + part
        out_ref[...] = total.astype(BF16)


def partial_sums(a_pieces, w_pieces):
    return pl.pallas_call(
        partial_body,
        in_specs=[pl.BlockSpec(memory_space=pltpu.VMEM)] * (RING + N_CTX),
        out_specs=[pl.BlockSpec(memory_space=pltpu.VMEM)] * RING,
        out_shape=[jax.ShapeDtypeStruct((BLOCK, COLS), BF16)] * RING,
        compiler_params=pltpu.CompilerParams(vmem_limit_bytes=VMEM_BYTES),
        cost_estimate=pl.CostEstimate(
            flops=2 * BLOCK * 1024 * 1536, bytes_accessed=5_000_000, transcendentals=0
        ),
        name="partial_sums",
    )(*a_pieces, *w_pieces)


def mid_body(*refs):
    sums, (resid_ref, hot_ref, mid_ref, send_ref) = refs[:RING], refs[RING:]
    proj = added(*[ref[...] for ref in sums])
    mid = (resid_ref[...].astype(F32) + proj).astype(BF16)
    mid_ref[...] = mid
    send_ref[...] = jnp.dot(hot_ref[...], mid, preferred_element_type=F32).astype(BF16)


def mid_and_slots(sums, resid_cols, hot):
    return pl.pallas_call(
        mid_body,
        in_specs=[pl.BlockSpec(memory_space=pltpu.VMEM)] * (RING + 2),
        out_specs=[pl.BlockSpec(memory_space=pltpu.VMEM)] * 2,
        out_shape=[
            jax.ShapeDtypeStruct((BLOCK, COLS), BF16),
            jax.ShapeDtypeStruct((N_EXP * ROWS, COLS), BF16),
        ],
        compiler_params=pltpu.CompilerParams(vmem_limit_bytes=VMEM_BYTES),
        cost_estimate=pl.CostEstimate(
            flops=2 * BLOCK * N_EXP * ROWS * COLS, bytes_accessed=3_000_000, transcendentals=0
        ),
        name="mid_and_slots",
    )(*sums, resid_cols, hot)


def sum_over_z(parts):
    far, after, ahead, own = parts
    return [own, along_z(far, 2), along_z(after, 1), along_z(ahead, -1)]


def added(*terms):
    total = terms[0].astype(F32)
    for term in terms[1:]:
        total = total + term.astype(F32)
    return total


def norm_body(got_ref, gain_ref, *out_refs):
    for half, out_ref in enumerate(out_refs):
        rows = pl.ds(half * HALF, HALF)
        total = jnp.zeros((HALF, 1), F32)
        for j in range(N_EXP):
            piece = got_ref[j, rows, :].astype(F32)
            total += jnp.sum(piece * piece, axis=1, keepdims=True)
        factor = lax.rsqrt(total * (1.0 / D) + EPS)
        for j in range(N_EXP):
            cols = pl.ds((j % RING * RING + j // RING) * COLS, COLS)
            piece = got_ref[j, rows, :].astype(F32)
            out_ref[:, cols] = (piece * factor * gain_ref[:, cols]).astype(BF16)


def norm_rows(got, mlp_gain):
    return pl.pallas_call(
        norm_body,
        in_specs=[pl.BlockSpec(memory_space=pltpu.VMEM)] * 2,
        out_specs=[pl.BlockSpec(memory_space=pltpu.VMEM)] * 2,
        out_shape=[jax.ShapeDtypeStruct((HALF, D), BF16)] * 2,
        compiler_params=pltpu.CompilerParams(vmem_limit_bytes=VMEM_BYTES),
        cost_estimate=pl.CostEstimate(
            flops=4 * ROWS * D, bytes_accessed=4 * ROWS * D, transcendentals=0
        ),
        name="norm_rows",
    )(got, mlp_gain.reshape(1, D))


STEPS = 3
WIDE = D // STEPS
PIECES = 2 * RING


def hidden_body(*refs):
    x_refs = refs[:PIECES]
    gate_ref, up_ref, out_ref, acc = refs[PIECES:]
    step = pl.program_id(0)
    ff = gate_ref.shape[1]
    rows = jnp.concatenate([r[...] for r in x_refs], axis=0)
    weight = jnp.concatenate([gate_ref[0], up_ref[0]], axis=0)
    part = lax.dot_general(
        rows, weight, (((1,), (1,)), ((), ())), preferred_element_type=F32
    )

    @pl.when(step == 0)
    def _():
        acc[...] = part

    @pl.when(step > 0)
    def _():
        acc[...] += part

    @pl.when(step == STEPS - 1)
    def _():
        out_ref[...] = (jax.nn.silu(acc[:, :ff]) * acc[:, ff:]).astype(BF16)


def hidden_rows(pieces, gate_w, up_w):
    ff = gate_w.shape[1]
    total = PIECES * HALF
    return pl.pallas_call(
        hidden_body,
        grid=(STEPS,),
        in_specs=[pl.BlockSpec((HALF, WIDE), lambda i: (0, i))] * PIECES
        + [pl.BlockSpec((1, ff, WIDE), lambda i: (0, 0, i))] * 2,
        out_specs=pl.BlockSpec((total, ff), lambda i: (0, 0)),
        out_shape=jax.ShapeDtypeStruct((total, ff), BF16),
        scratch_shapes=[pltpu.VMEM((total, 2 * ff), F32)],
        compiler_params=pltpu.CompilerParams(vmem_limit_bytes=VMEM_BYTES),
        cost_estimate=pl.CostEstimate(**LIGHT),
        name="hidden_rows",
    )(*pieces, gate_w, up_w)


def down_rows(hidden, down_w):
    return jnp.dot(hidden, down_w[0], preferred_element_type=F32).astype(BF16)


def both_cores(mine):
    return mine + [other_core(piece) for piece in mine]


def gather_halves(first, second):
    left, right = along_x(first, 1), along_x(first, -1)
    crossed = [other_core(first), other_core(second)]
    second, left, right, crossed = lax.optimization_barrier((second, left, right, crossed))
    far = along_x(left, 1)
    right_2 = along_x(second, -1)
    crossed += [other_core(left), other_core(right)]
    second, far, right_2, crossed = lax.optimization_barrier((second, far, right_2, crossed))
    left_2 = along_x(second, 1)
    far_2 = along_x(right_2, -1)
    far_crossed, right_crossed = lax.optimization_barrier((other_core(far), other_core(right_2)))
    ahead = [first, left, right, far, crossed[0], crossed[2], crossed[3], far_crossed]
    behind = [second, left_2, right_2, far_2]
    behind += [crossed[1], None, right_crossed, None]
    return ahead, behind


def expert_sums(hidden, down_w):
    count = RING * HALF
    theirs = other_core(down_rows(hidden[count:], down_w))
    mine = down_rows(hidden[:count], down_w)
    mine, theirs = lax.optimization_barrier((mine, theirs))
    both = added(mine, theirs).astype(BF16)
    return [both[i * HALF : (i + 1) * HALF] for i in range(RING)]


def to_owners(rows):
    rows = rows.reshape(CAP // 2, N_EXP, D // 128, 128).transpose(1, 0, 2, 3)
    return rows.reshape(N_EXP, CAP // 2 * (D // 128), 128)


LANE_ROWS = D // 128
SLOTS = CAP // 2


def combine_body(ids_ref, slot_ref, route_ref, first_ref, second_ref, out_ref, moe, mid):
    tokens = out_ref.shape[0]
    span = COLS // 128
    for t in range(tokens):
        total = jnp.zeros((LANE_ROWS, 128), F32)
        for k in range(2):
            piece = ids_ref[t, k] * 2
            slot = slot_ref[t, k]
            low = slot < SLOTS
            at = jnp.where(low, slot, slot - SLOTS) * LANE_ROWS
            rows = pl.ds(pl.multiple_of(at, LANE_ROWS), LANE_ROWS)
            a = first_ref[piece, rows, :].astype(F32) + first_ref[piece + 1, rows, :].astype(F32)
            b = second_ref[piece, rows, :].astype(F32) + second_ref[piece + 1, rows, :].astype(F32)
            total = total + route_ref[t, k] * jnp.where(low, a, b)
        moe[pl.ds(t * LANE_ROWS, LANE_ROWS), :] = total
    for j in range(N_EXP):
        mid[pl.ds(j * LANE_ROWS, LANE_ROWS), :] = first_ref[
            j, pl.ds(SLOTS * LANE_ROWS, LANE_ROWS), :
        ].astype(F32)
    for b in range(LANE_ROWS):
        block, c = b // span, b % span
        j = block % RING * RING + block // RING
        own = mid[pl.ds(j * LANE_ROWS + c, tokens, stride=span), :]
        added_up = moe[pl.ds(b, tokens, stride=LANE_ROWS), :]
        out_ref[:, b * 128 : (b + 1) * 128] = (own + added_up).astype(BF16)


def combined(ids, slot, route, returned):
    tokens = ids.shape[0]
    vmem = pl.BlockSpec(memory_space=pltpu.VMEM)
    smem = pl.BlockSpec(memory_space=pltpu.SMEM)
    return pl.pallas_call(
        combine_body,
        in_specs=[smem] * 3 + [vmem] * 2,
        out_specs=vmem,
        out_shape=jax.ShapeDtypeStruct((tokens, D), BF16),
        scratch_shapes=[
            pltpu.VMEM((tokens * LANE_ROWS, 128), F32),
            pltpu.VMEM((N_EXP * LANE_ROWS, 128), F32),
        ],
        compiler_params=pltpu.CompilerParams(vmem_limit_bytes=VMEM_BYTES),
        cost_estimate=pl.CostEstimate(**LIGHT),
        name="combined",
    )(ids, slot, route, *returned)


def shards(
    q_act,
    k_act,
    v_act,
    log_forget,
    attn_gain,
    w_out,
    resid,
    mlp_gain,
    gate_w,
    up_w,
    down_w,
    expert_ids,
    gate_codes,
):
    tok_dev = resid.shape[0]
    attn_out, chip, arrived = attention(q_act, k_act, v_act, log_forget, attn_gain)
    me_ctx, me_exp, _ = lax.optimization_barrier(
        (lax.axis_index("ctx"), lax.axis_index("exp"), chip)
    )
    me_z, me_y = me_exp // RING, me_exp % RING
    eighth = lax.dynamic_slice_in_dim(w_out, me_ctx * EIGHTH, EIGHTH, 0)
    eighth = eighth.reshape(EIGHTH, N_EXP, COLS).transpose(1, 0, 2)
    block = lambda y, z: lax.dynamic_index_in_dim(
        eighth, (me_y + y) % RING * RING + (me_z + z) % RING, 0, keepdims=False
    )
    eighth = [
        jnp.concatenate([block(y, z) for z in range(RING)], axis=1) for y in range(RING)
    ]
    w_rows = jnp.concatenate(
        [eighth[0], along_y(eighth[1], 1), along_y(eighth[3], -1), along_y(eighth[2], 2)]
    )

    w_rows, arrived = lax.optimization_barrier((w_rows, arrived))
    w_left, w_right = along_x(w_rows, 1), along_x(w_rows, -1)
    a_pieces = [attn_out, along_y(attn_out, 1), along_y(attn_out, -1), along_y(attn_out, 2)]

    w_left, w_right, a_pieces[1:3] = lax.optimization_barrier((w_left, w_right, a_pieces[1:3]))
    w_half = w_rows.shape[0] // 2
    w_far = jnp.concatenate([along_x(w_left[:w_half], 1), along_x(w_right[w_half:], -1)])
    near = both_cores([w_rows, w_left, w_right])
    w_far, a_pieces = lax.optimization_barrier((w_far, a_pieces))
    w_pieces = near[:3] + [w_far] + near[3:] + [other_core(w_far)]

    parts = partial_sums(a_pieces, w_pieces)
    resid, expert_ids, _ = lax.optimization_barrier((resid, expert_ids, parts[0]))
    slot = slot_targets(expert_ids)
    blocks = resid.reshape(tok_dev, RING, RING, COLS).transpose(2, 1, 0, 3)
    named = (expert_ids * 8 + slot).T.reshape(1, -1).astype(BF16)
    named = jnp.pad(named, ((0, 7), (0, COLS - named.shape[1])))
    blocks = jnp.concatenate(
        [
            blocks.reshape(N_EXP, tok_dev, COLS),
            jnp.broadcast_to(named[None], (N_EXP,) + named.shape),
        ],
        axis=1,
    )
    blocks = all_to_all_exp(blocks)
    resid_cols = blocks[:, :tok_dev].reshape(N_EXP * tok_dev, COLS)
    named = blocks[:, tok_dev, : 2 * tok_dev].astype(jnp.int32)
    owner = jnp.arange(N_EXP, dtype=jnp.int32)[:, None]
    places = (named // 8 * CAP + named % 8) * N_EXP + owner
    places = places.reshape(N_EXP, 2, tok_dev).transpose(1, 0, 2).reshape(2, N_EXP * tok_dev)
    targets = jnp.arange(N_EXP * ROWS, dtype=jnp.int32)
    targets = (targets // (2 * ROWS)) * ROWS + targets % ROWS
    hot = (targets[:, None] == places[0][None]) | (targets[:, None] == places[1][None])
    hot = hot.astype(BF16)

    proj = sum_over_z(parts)
    mid_cols, send = mid_and_slots(proj, resid_cols, hot)
    got = all_to_all_exp(send.reshape(N_EXP, ROWS, COLS))
    halves = norm_rows(got, mlp_gain)
    ahead, behind = gather_halves(*halves)
    hidden = hidden_rows(ahead, gate_w, up_w)
    hidden, behind[1:4] = lax.optimization_barrier((hidden, behind[1:4]))
    own, left, right, far = expert_sums(hidden, down_w)
    behind[5], behind[7] = other_core(behind[1]), other_core(behind[3])
    behind[0], left, far = lax.optimization_barrier((behind[0], left, far))
    far, left = along_x(far, 1), along_x(left, -1)
    hidden = hidden_rows(behind, gate_w, up_w)
    hidden, far, left = lax.optimization_barrier((hidden, far, left))
    right = along_x(added(right, far).astype(BF16), 1)
    own_2, left_2, right_2, far_2 = expert_sums(hidden, down_w)
    part = HALF // 2
    up, down = along_x(far_2[:part], 1), along_x(far_2[part:], -1)
    sent = jnp.concatenate(
        [
            to_owners(added(own, left, right).astype(BF16)),
            mid_cols.reshape(N_EXP, tok_dev * COLS // 128, 128),
        ],
        axis=1,
    )
    returned = [all_to_all_exp(sent)]
    right_2 = jnp.concatenate([added(right_2[:part], up).astype(BF16), right_2[part:]])
    left_2 = jnp.concatenate([left_2[:part], added(left_2[part:], down).astype(BF16)])
    from_left, from_right = along_x(right_2, 1), along_x(left_2, -1)
    back = to_owners(added(own_2, from_left, from_right).astype(BF16))
    returned.append(all_to_all_exp(back))
    route = gate_codes.astype(F32)
    route = route / jnp.sum(route, axis=1, keepdims=True)
    return combined(expert_ids, slot, route, returned)


def solution(mesh):
    placed = (
        P("ctx", "exp"),
        P("ctx", "exp"),
        P("ctx", "exp"),
        P("exp", "ctx"),
        P("exp"),
        P("exp", None),
        P(("ctx", "exp"), None),
        P(),
        P("exp", "ctx", None),
        P("exp", "ctx", None),
        P("exp", "ctx", None),
        P(("ctx", "exp"), None),
        P(("ctx", "exp"), None),
    )
    return jax.shard_map(
        shards, mesh=mesh, in_specs=placed, out_specs=P(("ctx", "exp"), None), check_vma=False
    )
```
